256 devices in a mesh: expert: 64 (over z, y, x_hi), dp: 4 (over x_lo, core).
Axes of the slice: x: 4 (x_hi: 2, x_lo: 2; x = x_hi * 2 + x_lo), y: 4, z: 8, core: 2. Of those that a mesh axis runs over, the one named last changes fastest.
Arguments:
- tokens: bfloat16 [16384, 2048], P(('expert', 'dp')), may hold values from -6 to 6
- expert_ids: int32 [16384, 8], P(('expert', 'dp')), may hold values from 0 to 63, all different within a row; in each aligned block of 64 rows (0 to 63, 64 to 127, ...) at most 16 rows name the same one
- targets: bfloat16 [16384, 8, 2048], P(('expert', 'dp')), may hold values from -400 to 400
- gate_weight: bfloat16 [64, 2048, 768], P('expert', 'dp'), may hold values from -0.125 to 0.125
- up_weight: bfloat16 [64, 2048, 768], P('expert', 'dp'), may hold values from -0.125 to 0.125
- kept_units: int32 [64, 384], P('expert'), may hold values from 0 to 767, as said below
Outputs:
- refit: float32 [64, 384, 2048], P('expert', None, 'dp')
The draws below stay inside these ranges and needn't reach their ends.
Inputs may be any that keep to these rules, and one draw needn't show every extreme that they name: `expert_ids`: among the rows of one device no expert is named by more than 16 routes, and in every draw some device names some expert exactly 16 times. `kept_units`: each row holds 384 distinct hidden units in increasing order.
All inputs are finite; a program needn't handle non-finite values.
Results may differ from the reference program's by a relative error of at most 0.0034.
Values may be sent and summed in bfloat16 or wider, within the bound.
A program may use at most 128 MiB of HBM per device.

```python
import math
import jax
import jax.numpy as jnp
import numpy as np
from jax import lax

D = 2048
FF = 768
KEEP = 384
TOPK = 8
ITERS = 3
TOK_DEV = 64
EXPERTS = 64
TOKENS = 16384
CAP = 16


def draw_targets(key, part):
    key = jax.random.fold_in(key, 13)
    key_values, key_rows, key_cols = jax.random.split(key, 3)
    full_shape = (TOKENS, TOPK, D)
    row_scale = jnp.exp(jax.random.uniform(key_rows, (TOKENS, TOPK, 1), minval=math.log(0.5), maxval=math.log(2.0)))
    rising = 1.0 + 2.0 * jnp.arange(D, dtype=jnp.float32) / (D - 1)
    col_scale = jnp.exp(jax.random.uniform(key_cols, (D,), minval=math.log(0.5), maxval=math.log(2.0))) * rising
    values = jnp.clip(jax.random.normal(key_values, full_shape), -4.0, 4.0)
    return (8.0 * values * row_scale * col_scale).astype(jnp.bfloat16)


def draw_kept_units(key, part):
    key = jax.random.fold_in(key, 14)
    expert_keys = jax.random.split(key, EXPERTS)

    def choose_units(unit_key):
        return jnp.sort(jax.random.permutation(unit_key, FF)[:KEEP]).astype(jnp.int32)
    return jax.vmap(choose_units)(expert_keys)


def level_of(key, dims, cuts, least, top_value):
    def one(axis_at, blocks):
        draws = jax.random.uniform(jax.random.fold_in(jax.random.fold_in(key, 6), axis_at), (blocks,), jnp.float32, least / len(cuts), top_value / len(cuts))
        return jnp.repeat(jnp.exp(draws), dims[axis_at] // blocks).reshape((-1,) + (1,) * (len(dims) - axis_at - 1))

    level = one(*cuts[0])
    for cut in cuts[1:]:
        level = level * one(*cut)
    return level


def routed_block(stream_key, own, number, rows, count, top, reach, lean):
    ranking = jax.random.permutation(stream_key, count)
    packed, usual = shares(count, rows * top, reach, lean, True), shares(count, rows * top, reach, lean, False)
    places = jnp.arange(count)

    def named(sizes, rotation):
        used = int((sizes > 0).sum())
        fixed = max(1, used // 4)
        passed = fixed + (places - fixed + rotation * (used - fixed)) % max(1, count - fixed)
        return jnp.zeros((count,), jnp.int32).at[ranking[jnp.where(places < fixed, places, passed)]].set(jnp.asarray(sizes, jnp.int32))

    sizes = jnp.where(number % 4 == 0, named(packed, number // 4), named(usual, number - number // 4 - 1))
    mixed = jax.random.permutation(jax.random.fold_in(own, 3), count)
    source_of, taker = mixed[0:count // 2 * 2:2], mixed[1:count // 2 * 2:2]
    slack = jnp.minimum(sizes[source_of] - 1, reach - sizes[taker]) // 2
    slack = jnp.where((source_of == ranking[0]) | (taker == ranking[0]) | (sizes[taker] == 0), 0, jnp.maximum(slack, 0))
    passed = jax.random.randint(jax.random.fold_in(own, 4), (count // 2,), 0, 1 << 20) % (slack + 1)
    sizes = sizes.at[source_of].add(-passed).at[taker].add(passed)
    items = jnp.searchsorted(jnp.cumsum(sizes), jnp.arange(rows * top), side="right").astype(jnp.int32)
    table = items.reshape(top, rows).T
    table = table[jax.random.permutation(jax.random.fold_in(own, 1), rows)]
    rotation = jax.random.randint(jax.random.fold_in(own, 2), (rows, 1), 0, top)
    return jnp.take_along_axis(table, (jnp.arange(top)[None, :] + rotation) % top, axis=1)


def shares(amount, total, most, skew, full):
    weights = [(1 << 20) // math.isqrt(grade ** skew) + 1 for grade in range(1, amount + 1)]
    largest = most if full else min(most, max(-(-total // amount), total * weights[0] // sum(weights)))
    least = 1 if total - largest >= amount - 1 else 0
    given, spare = [largest] + [least] * (amount - 1), total - largest - least * (amount - 1)
    while spare > 0:
        candidates = [i for i in range(1, amount) if given[i] < largest] or [i for i in range(1, amount) if given[i] < most]
        pool, remaining = sum([weights[i] for i in candidates]), spare
        for i in candidates:
            more = min(most - given[i], max(1, remaining * weights[i] // pool), spare)
            given[i] = given[i] + more
            spare = spare - more
    return np.array(given)


def gaussian(own_key, dims, scale, most, cuts=(), kind=jnp.bfloat16):
    array = jax.random.normal(own_key, dims, jnp.float32) * scale
    if len(cuts) > 0:
        array = level_of(own_key, dims, cuts, -0.22, 0.18) * array
    return jnp.clip(array, min=-most, max=most).astype(kind)


def setup_inputs(seed: int = 0) -> dict:
    key_of = jax.random.split(jax.random.key(seed), 7)
    tokens = gaussian(key_of[0], (TOKENS, D), 1.0, 6.0, ((0, 256),))
    expert_ids_keys = jax.random.split(jax.random.fold_in(key_of[1], 1), TOKENS // TOK_DEV)
    expert_ids_turns = jax.random.permutation(jax.random.fold_in(key_of[1], 3), TOKENS // TOK_DEV)
    expert_ids = jax.vmap(lambda own, number: routed_block(jax.random.fold_in(key_of[1], 2), own, number, TOK_DEV, EXPERTS, TOPK, CAP, 1))(expert_ids_keys, expert_ids_turns).reshape((TOKENS, TOPK))
    targets = draw_targets(jax.random.fold_in(key_of[6], 71), 0)
    gate_weight = gaussian(key_of[3], (EXPERTS, D, FF), D ** -0.5, 0.125, ((0, 64), (1, 4)))
    up_weight = gaussian(key_of[4], (EXPERTS, D, FF), D ** -0.5, 0.125, ((0, 64), (1, 4)))
    kept_units = draw_kept_units(jax.random.fold_in(key_of[6], 71), 0)
    return dict(tokens=tokens, expert_ids=expert_ids, targets=targets, gate_weight=gate_weight, up_weight=up_weight, kept_units=kept_units)


def reference(tokens, expert_ids, targets, gate_weight, up_weight, kept_units):
    pair_total = TOKENS * TOPK
    most_rows = CAP * (TOKENS // TOK_DEV)
    flat_ids = expert_ids.reshape(-1).astype(jnp.int32)
    order = jnp.argsort(flat_ids, stable=True).astype(jnp.int32)
    sorted_ids = flat_ids[order]
    labels = jnp.arange(EXPERTS, dtype=jnp.int32)
    starts = jnp.searchsorted(sorted_ids, labels, side="left").astype(jnp.int32)
    finishes = jnp.searchsorted(sorted_ids, labels, side="right").astype(jnp.int32)
    padded = jnp.concatenate([order, jnp.zeros((most_rows,), jnp.int32)])
    target_table = targets.reshape(pair_total, D)

    def refit_expert(expert):
        pair_index = lax.dynamic_slice_in_dim(padded, starts[expert], most_rows)
        is_live = jnp.arange(most_rows, dtype=jnp.int32) < (finishes[expert] - starts[expert])
        token_data = jnp.where(is_live[:, None], tokens[pair_index // TOPK], 0).astype(jnp.bfloat16)
        goal_data = jnp.where(is_live[:, None], target_table[pair_index], 0).astype(jnp.bfloat16)
        kept_cols = kept_units[expert]
        gate_kept = jnp.take(gate_weight[expert], kept_cols, axis=1)
        up_kept = jnp.take(up_weight[expert], kept_cols, axis=1)
        gate_acts = jnp.dot(token_data, gate_kept, preferred_element_type=jnp.float32)
        up_acts = jnp.dot(token_data, up_kept, preferred_element_type=jnp.float32)
        hidden = (jax.nn.silu(gate_acts) * up_acts).astype(jnp.bfloat16)
        gram = jnp.dot(hidden.T, hidden, preferred_element_type=jnp.float32)
        rhs = jnp.dot(hidden.T, goal_data, preferred_element_type=jnp.float32)
        damping = 0.01 * (jnp.mean(jnp.diagonal(gram)) + 1e-6)
        system = gram + damping * jnp.eye(KEEP, dtype=jnp.float32)
        solution = jnp.zeros((KEEP, D), jnp.float32)
        residual = rhs
        direction = rhs
        norm_now = jnp.sum(residual * residual)
        for iteration in range(ITERS):
            applied = jnp.dot(system, direction, precision=lax.Precision.HIGHEST)
            step_size = norm_now / jnp.sum(direction * applied)
            solution = solution + step_size * direction
            residual = residual - step_size * applied
            norm_next = jnp.sum(residual * residual)
            direction = residual + (norm_next / norm_now) * direction
            norm_now = norm_next
        return solution

    return lax.map(refit_expert, jnp.arange(EXPERTS, dtype=jnp.int32))
```

```python
import functools

import jax
import jax.numpy as jnp
from jax import lax
from jax.experimental import pallas as pl
from jax.experimental.pallas import tpu as pltpu
from jax.sharding import PartitionSpec as P

ITERS = 3
Z, Y, H, L, C = 8, 4, 2, 2, 2
PLANE = Y * H
CAP = 16
MESH = pl.DeviceIdType.MESH
NT = (((1,), (1,)), ((), ()))


def dot(a, b, dims=(((1,), (0,)), ((), ()))):
    return lax.dot_general(a, b, dims, preferred_element_type=jnp.float32)


def kernel(
    ids_ref, kept_ref, tokens_hbm, targets_hbm, gate_hbm, up_hbm, out_ref,
    tok, idsb, targ, gate, up, slots, before, fsend, feats, weights, hid, tsend, tmid, tfin,
    rhs, system, vec_p, vec_s, scal,
    in_sem, ring_send, ring_recv, idr_send, idr_recv, f_send, f_recv, t1_send, t1_recv,
    t2_send, t2_recv, w_send, w_recv, h_send, h_recv, s_send, s_recv,
):
    e = lax.axis_index("expert")
    d = lax.axis_index("dp")
    z, y, h = e // PLANE, (e // H) % Y, e % H
    l, c = d // C, d % C
    here = y * H + h

    def at_z(o):
        return ((z + o) % Z) * PLANE + here, d

    def in_plane(k):
        y2, h2 = (y + k // 8) % Y, (h + (k // 4) % 2) % H
        l2, c2 = (l + (k // 2) % 2) % L, (c + k % 2) % C
        return y2 * H + h2, l2 * C + c2

    def remote(src, dst, send, recv, device):
        return pltpu.make_async_remote_copy(
            src_ref=src, dst_ref=dst, send_sem=send, recv_sem=recv, device_id=device, device_id_type=MESH
        )

    def drain(ref, sem):
        pltpu.make_async_copy(ref, ref, sem).wait()

    barrier = pltpu.get_barrier_semaphore()

    def greet_z(o, _):
        pl.semaphore_signal(barrier, inc=1, device_id=at_z(o), device_id_type=MESH)
        return 0

    def greet_plane(k, _):
        i2, d2 = in_plane(k)
        pl.semaphore_signal(barrier, inc=1, device_id=(z * PLANE + i2, d2), device_id_type=MESH)
        return 0

    lax.fori_loop(1, Z, greet_z, 0)
    lax.fori_loop(1, PLANE * L * C, greet_plane, 0)

    loads = [
        pltpu.make_async_copy(src, dst, in_sem.at[n])
        for n, (src, dst) in enumerate(
            [(tokens_hbm, tok.at[0]), (targets_hbm, targ), (gate_hbm, gate), (up_hbm, up)]
        )
    ]
    for load in loads:
        load.start()

    idsb[0] = jnp.broadcast_to(ids_ref[...], idsb.shape[1:])
    routes = idsb.shape[2]
    row_at = lax.broadcasted_iota(jnp.int32, (routes, routes), 0)
    col_at = lax.broadcasted_iota(jnp.int32, (routes, routes), 1)
    before[...] = (row_at < col_at).astype(jnp.float32).astype(jnp.bfloat16)

    def places(ids, first, count):
        named = (ids == first + lax.broadcasted_iota(jnp.int32, (count, routes), 0)).astype(jnp.float32)
        rank = dot(named.astype(jnp.bfloat16), before[...])
        return jnp.where(named > 0, rank, -1.0)

    def one_hot(place):
        wide = jnp.broadcast_to(place[:, None, :], (PLANE, CAP, routes))
        slot = lax.broadcasted_iota(jnp.int32, (PLANE, CAP, routes), 1).astype(jnp.float32)
        return (wide == slot).astype(jnp.float32).reshape(PLANE * CAP, routes).astype(jnp.bfloat16)

    ids_row = ids_ref[...]
    all_places = places(jnp.broadcast_to(ids_row, (Z * PLANE, routes)), 0, Z * PLANE)
    for n in range(Z):
        slots[n] = all_places[n * PLANE : (n + 1) * PLANE]

    pl.semaphore_wait(barrier, Z - 1 + PLANE * L * C - 1)
    loads[0].wait()

    half = tok.shape[1] // 2

    def ring_start(step):
        src_r, src_l = 2 * (step - 1), jnp.maximum(2 * step - 3, 0)
        remote(tok.at[src_r], tok.at[2 * step], ring_send, ring_recv.at[step, 0], at_z(1)).start()
        remote(tok.at[src_l], tok.at[2 * step - 1], ring_send, ring_recv.at[step, 1], at_z(Z - 1)).start()
        remote(idsb.at[src_r], idsb.at[2 * step], idr_send, idr_recv.at[step, 0], at_z(1)).start()
        remote(idsb.at[src_l], idsb.at[2 * step - 1], idr_send, idr_recv.at[step, 1], at_z(Z - 1)).start()

    def ring_wait(step):
        drain(tok.at[2 * step], ring_recv.at[step, 0])
        drain(tok.at[2 * step - 1], ring_recv.at[step, 1])
        drain(idsb.at[2 * step], idr_recv.at[step, 0])
        drain(idsb.at[2 * step - 1], idr_recv.at[step, 1])

    low, high = pl.ds(0, half), pl.ds(half, half)

    def ring_start_last():
        remote(tok.at[6, low], tok.at[7, low], ring_send, ring_recv.at[4, 0], at_z(1)).start()
        remote(tok.at[5, high], tok.at[7, high], ring_send, ring_recv.at[4, 1], at_z(Z - 1)).start()
        remote(idsb.at[6], idsb.at[7], idr_send, idr_recv.at[4, 0], at_z(1)).start()

    def ring_wait_last():
        drain(tok.at[7, low], ring_recv.at[4, 0])
        drain(tok.at[7, high], ring_recv.at[4, 1])
        drain(idsb.at[7], idr_recv.at[4, 0])

    def pack_features(s):
        place = places(idsb[s], z * PLANE, PLANE)
        tokens_of = (
            lax.broadcasted_iota(jnp.int32, (routes, tok.shape[1]), 0) // (routes // tok.shape[1])
            == lax.broadcasted_iota(jnp.int32, (routes, tok.shape[1]), 1)
        ).astype(jnp.float32).astype(jnp.bfloat16)
        picks = dot(one_hot(place), tokens_of).astype(jnp.bfloat16)
        fsend[s] = dot(picks, tok[s]).astype(jnp.bfloat16)

        def push(k, _):
            y2, h2 = (y + k // 2) % Y, (h + k % 2) % H
            d2 = ((l + k % 2) % L) * C + c
            i2 = y2 * H + h2
            rows = pl.ds(pl.multiple_of(i2 * CAP, CAP), CAP)
            mine = pl.ds(pl.multiple_of(here * CAP, CAP), CAP)
            remote(
                fsend.at[s, rows], feats.at[s, mine], f_send.at[s], f_recv.at[s], (z * PLANE + i2, d2)
            ).start()
            return 0

        lax.fori_loop(1, PLANE, push, 0)
        mine = pl.ds(pl.multiple_of(here * CAP, CAP), CAP)
        pltpu.make_async_copy(fsend.at[s, mine], feats.at[s, mine], f_recv.at[s]).start()

    def pack_targets(s, o):
        packed = dot(one_hot(slots[(z + o) % Z]), targ[...]).astype(jnp.bfloat16)
        width = tsend.shape[3]
        for n in range(L * C):
            tsend[s, n] = packed[:, n * width : (n + 1) * width]

    def hop_z(s, o, other):
        remote(tsend.at[s], tmid.at[other], t1_send.at[s], t1_recv.at[other], at_z(o)).start()

    def spread(src, s):
        def push(k, _):
            i2, d2 = in_plane(k)
            owner = ((l + (k // 4) % 2) % L) * C + c
            rows = pl.ds(pl.multiple_of(i2 * CAP, CAP), CAP)
            there = pl.ds(pl.multiple_of((owner * PLANE + here) * CAP, CAP), CAP)
            remote(
                src.at[s, d2, rows], tfin.at[s, there], t2_send.at[s], t2_recv.at[s], (z * PLANE + i2, d2)
            ).start()
            return 0

        lax.fori_loop(1, PLANE * L * C, push, 0)
        rows = pl.ds(pl.multiple_of(here * CAP, CAP), CAP)
        there = pl.ds(pl.multiple_of((d * PLANE + here) * CAP, CAP), CAP)
        pltpu.make_async_copy(src.at[s, d, rows], tfin.at[s, there], t2_recv.at[s]).start()

    across = (e, ((l + 1) % L) * C + c)
    beside = (e, l * C + (c + 1) % C)
    d_across = ((l + 1) % L) * C + c
    d_beside = l * C + (c + 1) % C
    d_diag = ((l + 1) % L) * C + (c + 1) % C

    ring_start(1)
    pack_features(0)
    loads[1].wait()
    pack_targets(0, 0)
    spread(tsend, 0)

    loads[2].wait()
    loads[3].wait()
    keep = kept_ref.shape[1]
    hidden_units = gate.shape[1]
    kept_down = jnp.transpose(jnp.broadcast_to(kept_ref[...].astype(jnp.float32), (128, keep)))
    lane = lax.broadcasted_iota(jnp.int32, (keep, 128), 1).astype(jnp.float32)
    chosen = jnp.concatenate(
        [(kept_down == lane + float(128 * n)).astype(jnp.float32) for n in range(hidden_units // 128)], axis=1
    ).astype(jnp.bfloat16)
    weights[d, pl.ds(0, keep)] = dot(chosen, gate[...], NT).astype(jnp.bfloat16)
    weights[d, pl.ds(keep, keep)] = dot(chosen, up[...], NT).astype(jnp.bfloat16)
    remote(weights.at[d], weights.at[d], w_send.at[0], w_recv.at[0], across).start()
    remote(weights.at[d], weights.at[d], w_send.at[1], w_recv.at[1], beside).start()

    def turn(step, _):
        ring_wait(step)

        @pl.when(step < 3)
        def _():
            ring_start(step + 1)

        @pl.when(step == 3)
        def _():
            ring_start_last()

        pack_features(2 * step - 1)
        pack_features(2 * step)
        pack_targets(2 * step - 1, step)
        hop_z(2 * step - 1, step, 2 * step)
        pack_targets(2 * step, Z - step)
        hop_z(2 * step, Z - step, 2 * step - 1)
        return 0

    lax.fori_loop(1, 4, turn, 0)
    ring_wait_last()
    pack_features(7)
    pack_targets(7, Z // 2)
    hop_z(7, Z // 2, 7)

    drain(weights.at[d_across], w_recv.at[0])
    remote(weights.at[d_across], weights.at[d_across], w_send.at[2], w_recv.at[2], beside).start()

    def forward(s, _):
        drain(tmid.at[s], t1_recv.at[s])
        spread(tmid, s)
        return 0

    lax.fori_loop(1, 5, forward, 0)

    drain(weights.at[d_beside], w_recv.at[1])
    drain(weights.at[d_diag], w_recv.at[2])

    def activate(n, _):
        drain(feats.at[2 * n], f_recv.at[2 * n])
        drain(feats.at[2 * n + 1], f_recv.at[2 * n + 1])
        rows = feats.shape[1]
        block = feats[pl.ds(2 * n, 2)].reshape(2 * rows, feats.shape[2])
        width = weights.shape[2]
        acts = dot(weights[0], block[:, 0:width], NT)
        for q in range(1, L * C):
            acts = acts + dot(weights[q], block[:, q * width : (q + 1) * width], NT)
        gate_acts, up_acts = acts[:keep], acts[keep:]
        hidden = (gate_acts / (1.0 + jnp.exp(-gate_acts)) * up_acts).astype(jnp.bfloat16)
        hid[d, 2 * n] = hidden[:, :rows]
        hid[d, 2 * n + 1] = hidden[:, rows:]
        return 0

    lax.fori_loop(0, 4, activate, 0)
    remote(hid.at[d], hid.at[d], h_send.at[0], h_recv.at[0], across).start()
    remote(hid.at[d], hid.at[d], h_send.at[1], h_recv.at[1], beside).start()

    lax.fori_loop(5, 7, forward, 0)
    drain(hid.at[d_across], h_recv.at[0])
    remote(hid.at[d_across], hid.at[d_across], h_send.at[2], h_recv.at[2], beside).start()
    forward(7, 0)
    drain(hid.at[d_beside], h_recv.at[1])
    drain(hid.at[d_diag], h_recv.at[2])

    def hidden_of(s):
        return jnp.concatenate([hid[q, s] for q in range(L * C)], axis=1)

    system[...] = jnp.zeros_like(system)

    def add_gram(s, _):
        block = hidden_of(s)
        system[...] += dot(block, block, NT)
        return 0

    lax.fori_loop(0, Z, add_gram, 0)
    gram = system[...]
    on_diagonal = lax.broadcasted_iota(jnp.int32, gram.shape, 0) == lax.broadcasted_iota(jnp.int32, gram.shape, 1)
    trace = jnp.sum(jnp.where(on_diagonal, gram, 0.0))
    damping = 0.01 * (trace / keep + 1e-6)
    system[...] = gram + jnp.where(on_diagonal, damping, 0.0)

    rhs[...] = jnp.zeros_like(rhs)

    def add_rhs(s, _):
        drain(tfin.at[s], t2_recv.at[s])
        rhs[...] += dot(hidden_of(s), tfin[s])
        return 0

    lax.fori_loop(0, Z, add_rhs, 0)

    def folded(value):
        rows = value.reshape(value.shape[0] // 8, 8, value.shape[1]).sum(axis=0)
        total = rows[:, 0:128]
        for n in range(1, value.shape[1] // 128):
            total = total + rows[:, n * 128 : (n + 1) * 128]
        return total

    def exchange(it, first, second):
        scal[it, d, 0] = first
        scal[it, d, 1] = second
        copies = []
        for k in range(1, L * C):
            there = (d + k) % (L * C)
            copies.append(
                remote(scal.at[it, d], scal.at[it, d], s_send.at[it, k], s_recv.at[it, k], (e, there))
            )
        for copy in copies:
            copy.start()
        for copy in copies:
            copy.wait()
        sums = scal[it, 0]
        for k in range(1, L * C):
            sums = sums + scal[it, k]
        return jnp.sum(sums[0]), jnp.sum(sums[1])

    rr_old = alpha = None
    for it in range(ITERS):
        residual = rhs[...]
        image = jnp.dot(system[...], residual, precision=lax.Precision.HIGHEST)
        rr, curve = exchange(it, folded(residual * residual), folded(residual * image))
        if it == 0:
            alpha = rr / curve
            vec_p[...] = residual
            vec_s[...] = image
            out_ref[0] = alpha * residual
            rhs[...] = residual - alpha * image
        else:
            beta = rr / rr_old
            alpha = rr / (curve - beta * rr / alpha)
            direction = residual + beta * vec_p[...]
            out_ref[0] += alpha * direction
            if it + 1 < ITERS:
                applied = image + beta * vec_s[...]
                vec_p[...] = direction
                vec_s[...] = applied
                rhs[...] = residual - alpha * applied
        rr_old = rr

    drain(tok.at[pl.ds(0, 7)], ring_send)
    drain(idsb.at[pl.ds(0, 7)], idr_send)
    for s in range(Z):
        drain(feats.at[s, pl.ds(0, (PLANE - 1) * CAP)], f_send.at[s])
        drain(tfin.at[s, pl.ds(0, (PLANE * L * C - 1) * CAP)], t2_send.at[s])
        if s:
            drain(tsend.at[s], t1_send.at[s])
    for n in range(3):
        drain(weights.at[0], w_send.at[n])
        drain(hid.at[0], h_send.at[n])


def body(tokens, expert_ids, targets, gate_weight, up_weight, kept_units):
    tok_rows, model_width = tokens.shape
    routes = expert_ids.shape[1]
    keep = kept_units.shape[1]
    rows, units = gate_weight.shape[1:]
    ids = expert_ids.reshape(1, -1)
    targets = targets.reshape(-1, model_width)
    part = L * C
    out_cols = model_width // part
    slots = PLANE * CAP
    vmem = pl.BlockSpec(memory_space=pltpu.VMEM)
    hbm = pl.BlockSpec(memory_space=pl.ANY)
    dma = pltpu.SemaphoreType.DMA
    bf, f32 = jnp.bfloat16, jnp.float32
    return pl.pallas_call(
        kernel,
        out_shape=jax.ShapeDtypeStruct((1, keep, out_cols), f32),
        in_specs=[vmem, vmem, hbm, hbm, hbm, hbm],
        out_specs=vmem,
        scratch_shapes=[
            pltpu.VMEM((Z, tok_rows, model_width), bf),
            pltpu.VMEM((Z, 8, tok_rows * routes), jnp.int32),
            pltpu.VMEM((tok_rows * routes, model_width), bf),
            pltpu.VMEM((rows, units), bf),
            pltpu.VMEM((rows, units), bf),
            pltpu.VMEM((Z, PLANE, tok_rows * routes), f32),
            pltpu.VMEM((tok_rows * routes, tok_rows * routes), bf),
            pltpu.VMEM((Z, slots, model_width), bf),
            pltpu.VMEM((Z, slots, model_width), bf),
            pltpu.VMEM((part, 2 * keep, rows), bf),
            pltpu.VMEM((part, Z, keep, slots), bf),
            pltpu.VMEM((Z, part, slots, out_cols), bf),
            pltpu.VMEM((Z, part, slots, out_cols), bf),
            pltpu.VMEM((Z, part * slots, out_cols), bf),
            pltpu.VMEM((keep, out_cols), f32),
            pltpu.VMEM((keep, keep), f32),
            pltpu.VMEM((keep, out_cols), f32),
            pltpu.VMEM((keep, out_cols), f32),
            pltpu.VMEM((ITERS, part, 2, 8, 128), f32),
            dma((4,)), dma, dma((5, 2)), dma, dma((5, 2)), dma((Z,)), dma((Z,)), dma((Z,)), dma((Z,)),
            dma((Z,)), dma((Z,)), dma((3,)), dma((3,)), dma((3,)), dma((3,)),
            dma((ITERS, part)), dma((ITERS, part)),
        ],
        compiler_params=pltpu.CompilerParams(
            collective_id=0, has_side_effects=True, vmem_limit_bytes=56 * 2**20
        ),
    )(ids, kept_units, tokens, targets, gate_weight[0], up_weight[0])


def solution(mesh):
    placed = (
        P(("expert", "dp"), None),
        P(("expert", "dp"), None),
        P(("expert", "dp"), None, None),
        P("expert", "dp", None),
        P("expert", "dp", None),
        P("expert", None),
    )
    return jax.shard_map(
        body, mesh=mesh, in_specs=placed, out_specs=P("expert", None, "dp"), check_vma=False
    )
```

```python
import functools

import jax
import jax.numpy as jnp
from jax import lax
from jax.experimental import pallas as pl
from jax.experimental.pallas import tpu as pltpu
from jax.sharding import PartitionSpec as P

ITERS = 3
Z, Y, H, L, C = 8, 4, 2, 2, 2
PLANE = Y * H
CAP = 16
MESH = pl.DeviceIdType.MESH
NT = (((1,), (1,)), ((), ()))


def dot(a, b, dims=(((1,), (0,)), ((), ()))):
    return lax.dot_general(a, b, dims, preferred_element_type=jnp.float32)


def kernel(
    limits, ids_ref, kept_ref, tokens_hbm, targets_hbm, gate_hbm, up_hbm, out_ref, flag_ref,
    tok, idsb, targ, gate, up, before, fsend, feats, weights, hid, tsend, tmid, tpack, tfin,
    picked, rhs, system, vec_p, vec_s, scal, flags,
    in_sem, ring_send, ring_recv, idr_send, idr_recv, f_send, f_recv, t1_send, t1_recv,
    t2_send, t2_recv, w_send, w_recv, h_send, h_recv, s_send, s_recv, g_send, g_recv,
):
    most, spare = limits
    tokens_here = tokens_hbm.shape[0]
    e = lax.axis_index("expert")
    d = lax.axis_index("dp")
    z, y, h = e // PLANE, (e // H) % Y, e % H
    l, c = d // C, d % C
    here = y * H + h

    def at_z(o):
        return ((z + o) % Z) * PLANE + here, d

    def in_plane(k):
        y2, h2 = (y + k // 8) % Y, (h + (k // 4) % 2) % H
        l2, c2 = (l + (k // 2) % 2) % L, (c + k % 2) % C
        return y2 * H + h2, l2 * C + c2

    def remote(src, dst, send, recv, device):
        return pltpu.make_async_remote_copy(
            src_ref=src, dst_ref=dst, send_sem=send, recv_sem=recv, device_id=device, device_id_type=MESH
        )

    def drain(ref, sem):
        pltpu.make_async_copy(ref, ref, sem).wait()

    barrier = pltpu.get_barrier_semaphore()

    def greet_z(o, _):
        pl.semaphore_signal(barrier, inc=1, device_id=at_z(o), device_id_type=MESH)
        return 0

    def greet_plane(k, _):
        i2, d2 = in_plane(k)
        pl.semaphore_signal(barrier, inc=1, device_id=(z * PLANE + i2, d2), device_id_type=MESH)
        return 0

    lax.fori_loop(1, Z, greet_z, 0)
    lax.fori_loop(1, PLANE * L * C, greet_plane, 0)

    loads = [
        pltpu.make_async_copy(src, dst, in_sem.at[n])
        for n, (src, dst) in enumerate(
            [(tokens_hbm, tok.at[0, pl.ds(0, tokens_here)]), (targets_hbm, targ), (gate_hbm, gate), (up_hbm, up)]
        )
    ]
    for load in loads:
        load.start()

    idsb[0] = jnp.broadcast_to(ids_ref[...], idsb.shape[1:])
    routes = idsb.shape[2]
    row_at = lax.broadcasted_iota(jnp.int32, (routes, routes), 0)
    col_at = lax.broadcasted_iota(jnp.int32, (routes, routes), 1)
    before[...] = (row_at < col_at).astype(jnp.float32).astype(jnp.bfloat16)

    def places(ids, first, count):
        named = (ids == first + lax.broadcasted_iota(jnp.int32, (count, routes), 0)).astype(jnp.float32)
        rank = dot(named.astype(jnp.bfloat16), before[...])
        return jnp.where(named > 0, rank, -1.0)

    def one_hot(place):
        wide = jnp.broadcast_to(place[:, None, :], (PLANE, CAP, routes))
        slot = lax.broadcasted_iota(jnp.int32, (PLANE, CAP, routes), 1).astype(jnp.float32)
        return (wide == slot).astype(jnp.float32).reshape(PLANE * CAP, routes).astype(jnp.bfloat16)

    def plane_rows(ids):
        plane = ids // PLANE
        named = (plane == lax.broadcasted_iota(jnp.int32, (Z, routes), 0)).astype(jnp.float32)
        rank = dot(named.astype(jnp.bfloat16), before[...])
        rank = jnp.broadcast_to(jnp.sum(named * rank, axis=0, keepdims=True), (Z, routes))
        over = (rank >= most).astype(jnp.float32)
        late = dot(over.astype(jnp.bfloat16), before[...])
        return plane, jnp.where(over > 0, most + late, rank), jnp.sum(over[0:1])

    def row_hot(place, first, count):
        row = first + lax.broadcasted_iota(jnp.int32, (count, routes), 0).astype(jnp.float32)
        return (jnp.broadcast_to(place[0:1], (count, routes)) == row).astype(jnp.float32).astype(jnp.bfloat16)

    my_plane, my_row, _ = plane_rows(idsb[0])
    flags[0] = jnp.zeros_like(flags[0])
    loads[1].wait()
    if spare:
        late_rows = pl.ds(tokens_here, spare)
        tok[0, late_rows] = dot(row_hot(my_row, float(most), spare), targ[...]).astype(jnp.bfloat16)

    pl.semaphore_wait(barrier, Z - 1 + PLANE * L * C - 1)
    loads[0].wait()

    half = tok.shape[1] // 2

    def ring_start(step):
        src_r, src_l = 2 * (step - 1), jnp.maximum(2 * step - 3, 0)
        remote(tok.at[src_r], tok.at[2 * step], ring_send, ring_recv.at[step, 0], at_z(1)).start()
        remote(tok.at[src_l], tok.at[2 * step - 1], ring_send, ring_recv.at[step, 1], at_z(Z - 1)).start()
        remote(idsb.at[src_r], idsb.at[2 * step], idr_send, idr_recv.at[step, 0], at_z(1)).start()
        remote(idsb.at[src_l], idsb.at[2 * step - 1], idr_send, idr_recv.at[step, 1], at_z(Z - 1)).start()

    def ring_wait(step):
        drain(tok.at[2 * step], ring_recv.at[step, 0])
        drain(tok.at[2 * step - 1], ring_recv.at[step, 1])
        drain(idsb.at[2 * step], idr_recv.at[step, 0])
        drain(idsb.at[2 * step - 1], idr_recv.at[step, 1])

    low, high = pl.ds(0, half), pl.ds(half, half)

    def ring_start_last():
        remote(tok.at[6, low], tok.at[7, low], ring_send, ring_recv.at[4, 0], at_z(1)).start()
        remote(tok.at[5, high], tok.at[7, high], ring_send, ring_recv.at[4, 1], at_z(Z - 1)).start()
        remote(idsb.at[6], idsb.at[7], idr_send, idr_recv.at[4, 0], at_z(1)).start()

    def ring_wait_last():
        drain(tok.at[7, low], ring_recv.at[4, 0])
        drain(tok.at[7, high], ring_recv.at[4, 1])
        drain(idsb.at[7], idr_recv.at[4, 0])

    def pack_features(s):
        place = places(idsb[s], z * PLANE, PLANE)
        hot = one_hot(place)
        tokens_of = (
            lax.broadcasted_iota(jnp.int32, (routes, tokens_here), 0) // (routes // tokens_here)
            == lax.broadcasted_iota(jnp.int32, (routes, tokens_here), 1)
        ).astype(jnp.float32).astype(jnp.bfloat16)
        picks = dot(hot, tokens_of).astype(jnp.bfloat16)
        fsend[s] = dot(picks, tok[s, pl.ds(0, tokens_here)]).astype(jnp.bfloat16)

        def push(k, _):
            y2, h2 = (y + k // 2) % Y, (h + k % 2) % H
            d2 = ((l + k % 2) % L) * C + c
            i2 = y2 * H + h2
            rows = pl.ds(pl.multiple_of(i2 * CAP, CAP), CAP)
            mine = pl.ds(pl.multiple_of(here * CAP, CAP), CAP)
            remote(
                fsend.at[s, rows], feats.at[s, mine], f_send.at[s], f_recv.at[s], (z * PLANE + i2, d2)
            ).start()
            return 0

        lax.fori_loop(1, PLANE, push, 0)
        mine = pl.ds(pl.multiple_of(here * CAP, CAP), CAP)
        pltpu.make_async_copy(fsend.at[s, mine], feats.at[s, mine], f_recv.at[s]).start()
        plane, row, late = plane_rows(idsb[s])
        picked[s] = dot(hot, row_hot(jnp.where(plane == z, row, -1.0), 0.0, most + spare), NT).astype(jnp.bfloat16)
        flags[0] = jnp.maximum(flags[0], late - float(spare))
        return hot

    def pack_targets(s, o):
        place = jnp.where(my_plane == (z + o) % Z, my_row, -1.0)
        tsend[s] = dot(row_hot(place, 0.0, most), targ[...]).astype(jnp.bfloat16)

    def hop_z(s, o, other):
        remote(tsend.at[s], tmid.at[other], t1_send.at[s], t1_recv.at[other], at_z(o)).start()

    def spread(s, packed):
        width = tpack.shape[3]
        for n in range(L * C):
            tpack[s, n] = packed[:, n * width : (n + 1) * width].astype(jnp.bfloat16)

        def push(k, _):
            i2, d2 = in_plane(k)
            owner = ((l + (k // 4) % 2) % L) * C + c
            rows = pl.ds(pl.multiple_of(i2 * CAP, CAP), CAP)
            there = pl.ds(pl.multiple_of((owner * PLANE + here) * CAP, CAP), CAP)
            remote(
                tpack.at[s, d2, rows], tfin.at[s, there], t2_send.at[s], t2_recv.at[s], (z * PLANE + i2, d2)
            ).start()
            return 0

        lax.fori_loop(1, PLANE * L * C, push, 0)
        rows = pl.ds(pl.multiple_of(here * CAP, CAP), CAP)
        there = pl.ds(pl.multiple_of((d * PLANE + here) * CAP, CAP), CAP)
        pltpu.make_async_copy(tpack.at[s, d, rows], tfin.at[s, there], t2_recv.at[s]).start()

    across = (e, ((l + 1) % L) * C + c)
    beside = (e, l * C + (c + 1) % C)
    d_across = ((l + 1) % L) * C + c
    d_beside = l * C + (c + 1) % C
    d_diag = ((l + 1) % L) * C + (c + 1) % C

    ring_start(1)
    spread(0, dot(pack_features(0), targ[...]))

    loads[2].wait()
    loads[3].wait()
    keep = kept_ref.shape[1]
    hidden_units = gate.shape[1]
    kept_down = jnp.transpose(jnp.broadcast_to(kept_ref[...].astype(jnp.float32), (128, keep)))
    lane = lax.broadcasted_iota(jnp.int32, (keep, 128), 1).astype(jnp.float32)
    chosen = jnp.concatenate(
        [(kept_down == lane + float(128 * n)).astype(jnp.float32) for n in range(hidden_units // 128)], axis=1
    ).astype(jnp.bfloat16)
    weights[d, pl.ds(0, keep)] = dot(chosen, gate[...], NT).astype(jnp.bfloat16)
    weights[d, pl.ds(keep, keep)] = dot(chosen, up[...], NT).astype(jnp.bfloat16)
    remote(weights.at[d], weights.at[d], w_send.at[0], w_recv.at[0], across).start()
    remote(weights.at[d], weights.at[d], w_send.at[1], w_recv.at[1], beside).start()

    def turn(step, _):
        ring_wait(step)

        @pl.when(step < 3)
        def _():
            ring_start(step + 1)

        @pl.when(step == 3)
        def _():
            ring_start_last()

        pack_features(2 * step - 1)
        pack_features(2 * step)
        pack_targets(2 * step - 1, step)
        hop_z(2 * step - 1, step, 2 * step)
        pack_targets(2 * step, Z - step)
        hop_z(2 * step, Z - step, 2 * step - 1)
        return 0

    lax.fori_loop(1, 4, turn, 0)
    ring_wait_last()
    pack_features(7)
    pack_targets(7, Z // 2)
    hop_z(7, Z // 2, 7)

    drain(weights.at[d_across], w_recv.at[0])
    remote(weights.at[d_across], weights.at[d_across], w_send.at[2], w_recv.at[2], beside).start()

    def forward(s, _):
        drain(tmid.at[s], t1_recv.at[s])
        rows = tmid[s]
        if spare:
            rows = jnp.concatenate([rows, tok[s, late_rows]], axis=0)
        spread(s, dot(picked[s], rows))
        return 0

    lax.fori_loop(1, 5, forward, 0)

    drain(weights.at[d_beside], w_recv.at[1])
    drain(weights.at[d_diag], w_recv.at[2])

    def activate(n, _):
        drain(feats.at[2 * n], f_recv.at[2 * n])
        drain(feats.at[2 * n + 1], f_recv.at[2 * n + 1])
        rows = feats.shape[1]
        block = feats[pl.ds(2 * n, 2)].reshape(2 * rows, feats.shape[2])
        width = weights.shape[2]
        acts = dot(weights[0], block[:, 0:width], NT)
        for q in range(1, L * C):
            acts = acts + dot(weights[q], block[:, q * width : (q + 1) * width], NT)
        gate_acts, up_acts = acts[:keep], acts[keep:]
        hidden = (gate_acts / (1.0 + jnp.exp(-gate_acts)) * up_acts).astype(jnp.bfloat16)
        hid[d, 2 * n] = hidden[:, :rows]
        hid[d, 2 * n + 1] = hidden[:, rows:]
        return 0

    lax.fori_loop(0, 4, activate, 0)
    remote(hid.at[d], hid.at[d], h_send.at[0], h_recv.at[0], across).start()
    remote(hid.at[d], hid.at[d], h_send.at[1], h_recv.at[1], beside).start()

    lax.fori_loop(5, 7, forward, 0)
    drain(hid.at[d_across], h_recv.at[0])
    remote(hid.at[d_across], hid.at[d_across], h_send.at[2], h_recv.at[2], beside).start()
    forward(7, 0)

    def tell(k, _):
        i2, d2 = in_plane(k)
        remote(flags.at[0], flags.at[k], g_send, g_recv, (z * PLANE + i2, d2)).start()
        return 0

    lax.fori_loop(1, PLANE * L * C, tell, 0)
    drain(hid.at[d_beside], h_recv.at[1])
    drain(hid.at[d_diag], h_recv.at[2])

    def hidden_of(s):
        return jnp.concatenate([hid[q, s] for q in range(L * C)], axis=1)

    system[...] = jnp.zeros_like(system)

    def add_gram(s, _):
        block = hidden_of(s)
        system[...] += dot(block, block, NT)
        return 0

    lax.fori_loop(0, Z, add_gram, 0)
    gram = system[...]
    on_diagonal = lax.broadcasted_iota(jnp.int32, gram.shape, 0) == lax.broadcasted_iota(jnp.int32, gram.shape, 1)
    trace = jnp.sum(jnp.where(on_diagonal, gram, 0.0))
    damping = 0.01 * (trace / keep + 1e-6)
    system[...] = gram + jnp.where(on_diagonal, damping, 0.0)

    rhs[...] = jnp.zeros_like(rhs)

    def add_rhs(s, _):
        drain(tfin.at[s], t2_recv.at[s])
        rhs[...] += dot(hidden_of(s), tfin[s])
        return 0

    lax.fori_loop(0, Z, add_rhs, 0)

    def folded(value):
        rows = value.reshape(value.shape[0] // 8, 8, value.shape[1]).sum(axis=0)
        total = rows[:, 0:128]
        for n in range(1, value.shape[1] // 128):
            total = total + rows[:, n * 128 : (n + 1) * 128]
        return total

    def exchange(it, first, second):
        scal[it, d, 0] = first
        scal[it, d, 1] = second
        copies = []
        for k in range(1, L * C):
            there = (d + k) % (L * C)
            copies.append(
                remote(scal.at[it, d], scal.at[it, d], s_send.at[it, k], s_recv.at[it, k], (e, there))
            )
        for copy in copies:
            copy.start()
        for copy in copies:
            copy.wait()
        sums = scal[it, 0]
        for k in range(1, L * C):
            sums = sums + scal[it, k]
        return jnp.sum(sums[0]), jnp.sum(sums[1])

    rr_old = alpha = None
    for it in range(ITERS):
        residual = rhs[...]
        image = jnp.dot(system[...], residual, precision=lax.Precision.HIGHEST)
        rr, curve = exchange(it, folded(residual * residual), folded(residual * image))
        if it == 0:
            alpha = rr / curve
            vec_p[...] = residual
            vec_s[...] = image
            out_ref[0] = alpha * residual
            rhs[...] = residual - alpha * image
        else:
            beta = rr / rr_old
            alpha = rr / (curve - beta * rr / alpha)
            direction = residual + beta * vec_p[...]
            out_ref[0] += alpha * direction
            if it + 1 < ITERS:
                applied = image + beta * vec_s[...]
                vec_p[...] = direction
                vec_s[...] = applied
                rhs[...] = residual - alpha * applied
        rr_old = rr

    others = flags.at[pl.ds(1, PLANE * L * C - 1)]
    drain(others, g_recv)
    drain(others, g_send)
    flag_ref[...] = jnp.max(flags[...], axis=0)

    drain(tok.at[pl.ds(0, 7)], ring_send)
    drain(idsb.at[pl.ds(0, 7)], idr_send)
    for s in range(Z):
        drain(feats.at[s, pl.ds(0, (PLANE - 1) * CAP)], f_send.at[s])
        drain(tfin.at[s, pl.ds(0, (PLANE * L * C - 1) * CAP)], t2_send.at[s])
        if s:
            drain(tsend.at[s], t1_send.at[s])
    for n in range(3):
        drain(weights.at[0], w_send.at[n])
        drain(hid.at[0], h_send.at[n])


def refit(limits, number, tokens, expert_ids, targets, gate_weight, up_weight, kept_units):
    most, spare = limits
    tok_rows, model_width = tokens.shape
    routes = expert_ids.shape[1]
    keep = kept_units.shape[1]
    rows, units = gate_weight.shape[1:]
    ids = expert_ids.reshape(1, -1)
    targets = targets.reshape(-1, model_width)
    part = L * C
    out_cols = model_width // part
    slots = PLANE * CAP
    vmem = pl.BlockSpec(memory_space=pltpu.VMEM)
    hbm = pl.BlockSpec(memory_space=pl.ANY)
    dma = pltpu.SemaphoreType.DMA
    bf, f32 = jnp.bfloat16, jnp.float32
    return pl.pallas_call(
        functools.partial(kernel, limits),
        out_shape=(jax.ShapeDtypeStruct((1, keep, out_cols), f32), jax.ShapeDtypeStruct((8, 128), f32)),
        in_specs=[vmem, vmem, hbm, hbm, hbm, hbm],
        out_specs=(vmem, vmem),
        scratch_shapes=[
            pltpu.VMEM((Z, tok_rows + spare, model_width), bf),
            pltpu.VMEM((Z, 8, tok_rows * routes), jnp.int32),
            pltpu.VMEM((tok_rows * routes, model_width), bf),
            pltpu.VMEM((rows, units), bf),
            pltpu.VMEM((rows, units), bf),
            pltpu.VMEM((tok_rows * routes, tok_rows * routes), bf),
            pltpu.VMEM((Z, slots, model_width), bf),
            pltpu.VMEM((Z, slots, model_width), bf),
            pltpu.VMEM((part, 2 * keep, rows), bf),
            pltpu.VMEM((part, Z, keep, slots), bf),
            pltpu.VMEM((Z, most, model_width), bf),
            pltpu.VMEM((Z, most, model_width), bf),
            pltpu.VMEM((Z, part, slots, out_cols), bf),
            pltpu.VMEM((Z, part * slots, out_cols), bf),
            pltpu.VMEM((Z, slots, most + spare), bf),
            pltpu.VMEM((keep, out_cols), f32),
            pltpu.VMEM((keep, keep), f32),
            pltpu.VMEM((keep, out_cols), f32),
            pltpu.VMEM((keep, out_cols), f32),
            pltpu.VMEM((ITERS, part, 2, 8, 128), f32),
            pltpu.VMEM((PLANE * part, 8, 128), f32),
            dma((4,)), dma, dma((5, 2)), dma, dma((5, 2)), dma((Z,)), dma((Z,)), dma((Z,)), dma((Z,)),
            dma((Z,)), dma((Z,)), dma((3,)), dma((3,)), dma((3,)), dma((3,)),
            dma((ITERS, part)), dma((ITERS, part)), dma, dma,
        ],
        compiler_params=pltpu.CompilerParams(
            collective_id=number, has_side_effects=True, vmem_limit_bytes=56 * 2**20
        ),
    )(ids, kept_units, tokens, targets, gate_weight[0], up_weight[0])


def body(*args):
    result, flag = refit((80, 32), 0, *args)
    return lax.cond(flag[0, 0] > 0, lambda: refit((PLANE * CAP, 0), 1, *args)[0], lambda: result)


def solution(mesh):
    placed = (
        P(("expert", "dp"), None),
        P(("expert", "dp"), None),
        P(("expert", "dp"), None, None),
        P("expert", "dp", None),
        P("expert", "dp", None),
        P("expert", None),
    )
    return jax.shard_map(
        body, mesh=mesh, in_specs=placed, out_specs=P("expert", None, "dp"), check_vma=False
    )
```

```python
import functools

import jax
import jax.numpy as jnp
from jax import lax
from jax.experimental import pallas as pl
from jax.experimental.pallas import tpu as pltpu
from jax.sharding import PartitionSpec as P

ITERS = 3
Z, Y, H, L, C = 8, 4, 2, 2, 2
PLANE = Y * H
CAP = 16
MESH = pl.DeviceIdType.MESH
NT = (((1,), (1,)), ((), ()))


def dot(a, b, dims=(((1,), (0,)), ((), ()))):
    return lax.dot_general(a, b, dims, preferred_element_type=jnp.float32)


def kernel(
    limits, ids_ref, kept_ref, tokens_hbm, targets_hbm, gate_hbm, up_hbm, out_ref, flag_ref,
    tok, idsb, targ, gate, up, before, fsend, feats, weights, hid, tsend, tmid, tpack, tfin,
    picked, rhs, system, vec_p, vec_s, scal, flags,
    in_sem, ring_send, ring_recv, idr_send, idr_recv, f_send, f_recv, t1_send, t1_recv,
    t2_send, t2_recv, w_send, w_recv, h_send, h_recv, s_send, s_recv, g_send, g_recv,
):
    most, spare = limits
    tokens_here = tokens_hbm.shape[0]
    e = lax.axis_index("expert")
    d = lax.axis_index("dp")
    z, y, h = e // PLANE, (e // H) % Y, e % H
    l, c = d // C, d % C
    here = y * H + h

    def at_z(o):
        return ((z + o) % Z) * PLANE + here, d

    def in_plane(k):
        y2, h2 = (y + k // 8) % Y, (h + (k // 4) % 2) % H
        l2, c2 = (l + (k // 2) % 2) % L, (c + k % 2) % C
        return y2 * H + h2, l2 * C + c2

    def remote(src, dst, send, recv, device):
        return pltpu.make_async_remote_copy(
            src_ref=src, dst_ref=dst, send_sem=send, recv_sem=recv, device_id=device, device_id_type=MESH
        )

    def drain(ref, sem):
        pltpu.make_async_copy(ref, ref, sem).wait()

    barrier = pltpu.get_barrier_semaphore()

    def greet_z(o, _):
        pl.semaphore_signal(barrier, inc=1, device_id=at_z(o), device_id_type=MESH)
        return 0

    def greet_plane(k, _):
        i2, d2 = in_plane(k)
        pl.semaphore_signal(barrier, inc=1, device_id=(z * PLANE + i2, d2), device_id_type=MESH)
        return 0

    lax.fori_loop(1, Z, greet_z, 0)
    lax.fori_loop(1, PLANE * L * C, greet_plane, 0)

    loads = [
        pltpu.make_async_copy(src, dst, in_sem.at[n])
        for n, (src, dst) in enumerate(
            [(tokens_hbm, tok.at[0, pl.ds(0, tokens_here)]), (targets_hbm, targ), (gate_hbm, gate), (up_hbm, up)]
        )
    ]
    for load in loads:
        load.start()

    idsb[0] = jnp.broadcast_to(ids_ref[...], idsb.shape[1:])
    routes = idsb.shape[2]
    row_at = lax.broadcasted_iota(jnp.int32, (routes, routes), 0)
    col_at = lax.broadcasted_iota(jnp.int32, (routes, routes), 1)
    before[...] = (row_at < col_at).astype(jnp.float32).astype(jnp.bfloat16)

    def places(ids, first, count):
        named = (ids == first + lax.broadcasted_iota(jnp.int32, (count, routes), 0)).astype(jnp.float32)
        rank = dot(named.astype(jnp.bfloat16), before[...])
        return jnp.where(named > 0, rank, -1.0)

    def one_hot(place):
        wide = jnp.broadcast_to(place[:, None, :], (PLANE, CAP, routes))
        slot = lax.broadcasted_iota(jnp.int32, (PLANE, CAP, routes), 1).astype(jnp.float32)
        return (wide == slot).astype(jnp.float32).reshape(PLANE * CAP, routes).astype(jnp.bfloat16)

    def plane_rows(ids):
        plane = ids // PLANE
        named = (plane == lax.broadcasted_iota(jnp.int32, (Z, routes), 0)).astype(jnp.float32)
        rank = dot(named.astype(jnp.bfloat16), before[...])
        rank = jnp.broadcast_to(jnp.sum(named * rank, axis=0, keepdims=True), (Z, routes))
        over = (rank >= most).astype(jnp.float32)
        late = dot(over.astype(jnp.bfloat16), before[...])
        return plane, jnp.where(over > 0, most + late, rank), jnp.sum(over[0:1])

    def row_hot(place, first, count):
        row = first + lax.broadcasted_iota(jnp.int32, (count, routes), 0).astype(jnp.float32)
        return (jnp.broadcast_to(place[0:1], (count, routes)) == row).astype(jnp.float32).astype(jnp.bfloat16)

    my_plane, my_row, _ = plane_rows(idsb[0])
    flags[0] = jnp.zeros_like(flags[0])
    loads[1].wait()
    if spare:
        late_rows = pl.ds(tokens_here, spare)
        tok[0, late_rows] = dot(row_hot(my_row, float(most), spare), targ[...]).astype(jnp.bfloat16)

    pl.semaphore_wait(barrier, Z - 1 + PLANE * L * C - 1)
    loads[0].wait()

    half = tok.shape[1] // 2

    def ring_start(step):
        src_r, src_l = 2 * (step - 1), jnp.maximum(2 * step - 3, 0)
        remote(tok.at[src_r], tok.at[2 * step], ring_send, ring_recv.at[step, 0], at_z(1)).start()
        remote(tok.at[src_l], tok.at[2 * step - 1], ring_send, ring_recv.at[step, 1], at_z(Z - 1)).start()
        remote(idsb.at[src_r], idsb.at[2 * step], idr_send, idr_recv.at[step, 0], at_z(1)).start()
        remote(idsb.at[src_l], idsb.at[2 * step - 1], idr_send, idr_recv.at[step, 1], at_z(Z - 1)).start()

    def ring_wait(step):
        drain(tok.at[2 * step], ring_recv.at[step, 0])
        drain(tok.at[2 * step - 1], ring_recv.at[step, 1])
        drain(idsb.at[2 * step], idr_recv.at[step, 0])
        drain(idsb.at[2 * step - 1], idr_recv.at[step, 1])

    low, high = pl.ds(0, half), pl.ds(half, half)

    def ring_start_last():
        remote(tok.at[6, low], tok.at[7, low], ring_send, ring_recv.at[4, 0], at_z(1)).start()
        remote(tok.at[5, high], tok.at[7, high], ring_send, ring_recv.at[4, 1], at_z(Z - 1)).start()
        remote(idsb.at[6], idsb.at[7], idr_send, idr_recv.at[4, 0], at_z(1)).start()

    def ring_wait_last():
        drain(tok.at[7, low], ring_recv.at[4, 0])
        drain(tok.at[7, high], ring_recv.at[4, 1])
        drain(idsb.at[7], idr_recv.at[4, 0])

    def pack_features(s):
        place = places(idsb[s], z * PLANE, PLANE)
        hot = one_hot(place)
        tokens_of = (
            lax.broadcasted_iota(jnp.int32, (routes, tokens_here), 0) // (routes // tokens_here)
            == lax.broadcasted_iota(jnp.int32, (routes, tokens_here), 1)
        ).astype(jnp.float32).astype(jnp.bfloat16)
        picks = dot(hot, tokens_of).astype(jnp.bfloat16)
        fsend[s] = dot(picks, tok[s, pl.ds(0, tokens_here)]).astype(jnp.bfloat16)

        def push(k, _):
            y2, h2 = (y + k // 2) % Y, (h + k % 2) % H
            d2 = ((l + k % 2) % L) * C + c
            i2 = y2 * H + h2
            rows = pl.ds(pl.multiple_of(i2 * CAP, CAP), CAP)
            mine = pl.ds(pl.multiple_of(here * CAP, CAP), CAP)
            remote(
                fsend.at[s, rows], feats.at[s, mine], f_send.at[s], f_recv.at[s], (z * PLANE + i2, d2)
            ).start()
            return 0

        lax.fori_loop(1, PLANE, push, 0)
        mine = pl.ds(pl.multiple_of(here * CAP, CAP), CAP)
        pltpu.make_async_copy(fsend.at[s, mine], feats.at[s, mine], f_recv.at[s]).start()
        plane, row, late = plane_rows(idsb[s])
        picked[s] = dot(hot, row_hot(jnp.where(plane == z, row, -1.0), 0.0, most + spare), NT).astype(jnp.bfloat16)
        flags[0] = jnp.maximum(flags[0], late - float(spare))
        return hot

    def pack_targets(s, o):
        place = jnp.where(my_plane == (z + o) % Z, my_row, -1.0)
        tsend[s] = dot(row_hot(place, 0.0, most), targ[...]).astype(jnp.bfloat16)

    def hop_z(s, o, other):
        remote(tsend.at[s], tmid.at[other], t1_send.at[s], t1_recv.at[other], at_z(o)).start()

    def spread(s, packed):
        width = tpack.shape[3]
        for n in range(L * C):
            tpack[s, n] = packed[:, n * width : (n + 1) * width].astype(jnp.bfloat16)

        def push(k, _):
            i2, d2 = in_plane(k)
            owner = ((l + (k // 4) % 2) % L) * C + c
            rows = pl.ds(pl.multiple_of(i2 * CAP, CAP), CAP)
            there = pl.ds(pl.multiple_of((owner * PLANE + here) * CAP, CAP), CAP)
            remote(
                tpack.at[s, d2, rows], tfin.at[s, there], t2_send.at[s], t2_recv.at[s], (z * PLANE + i2, d2)
            ).start()
            return 0

        lax.fori_loop(1, PLANE * L * C, push, 0)
        rows = pl.ds(pl.multiple_of(here * CAP, CAP), CAP)
        there = pl.ds(pl.multiple_of((d * PLANE + here) * CAP, CAP), CAP)
        pltpu.make_async_copy(tpack.at[s, d, rows], tfin.at[s, there], t2_recv.at[s]).start()

    across = (e, ((l + 1) % L) * C + c)
    beside = (e, l * C + (c + 1) % C)
    d_across = ((l + 1) % L) * C + c
    d_beside = l * C + (c + 1) % C
    d_diag = ((l + 1) % L) * C + (c + 1) % C

    ring_start(1)
    spread(0, dot(pack_features(0), targ[...]))

    loads[2].wait()
    loads[3].wait()
    keep = kept_ref.shape[1]
    hidden_units = gate.shape[1]
    kept_down = jnp.transpose(jnp.broadcast_to(kept_ref[...].astype(jnp.float32), (128, keep)))
    lane = lax.broadcasted_iota(jnp.int32, (keep, 128), 1).astype(jnp.float32)
    chosen = jnp.concatenate(
        [(kept_down == lane + float(128 * n)).astype(jnp.float32) for n in range(hidden_units // 128)], axis=1
    ).astype(jnp.bfloat16)
    weights[d, pl.ds(0, keep)] = dot(chosen, gate[...], NT).astype(jnp.bfloat16)
    weights[d, pl.ds(keep, keep)] = dot(chosen, up[...], NT).astype(jnp.bfloat16)
    remote(weights.at[d], weights.at[d], w_send.at[0], w_recv.at[0], across).start()
    remote(weights.at[d], weights.at[d], w_send.at[1], w_recv.at[1], beside).start()

    def forward(s, _):
        drain(tmid.at[s], t1_recv.at[s])
        rows = tmid[s]
        if spare:
            rows = jnp.concatenate([rows, tok[s, late_rows]], axis=0)
        spread(s, dot(picked[s], rows))
        return 0

    def activate(n, _):
        drain(feats.at[2 * n], f_recv.at[2 * n])
        drain(feats.at[2 * n + 1], f_recv.at[2 * n + 1])
        rows = feats.shape[1]
        block = feats[pl.ds(2 * n, 2)].reshape(2 * rows, feats.shape[2])
        width = weights.shape[2]
        acts = dot(weights[0], block[:, 0:width], NT)
        for q in range(1, L * C):
            acts = acts + dot(weights[q], block[:, q * width : (q + 1) * width], NT)
        gate_acts, up_acts = acts[:keep], acts[keep:]
        hidden = (gate_acts / (1.0 + jnp.exp(-gate_acts)) * up_acts).astype(jnp.bfloat16)
        hid[d, 2 * n] = hidden[:, :rows]
        hid[d, 2 * n + 1] = hidden[:, rows:]
        part = hid.at[d, pl.ds(2 * n, 2)]
        remote(part, part, h_send.at[n, 0], h_recv.at[n, 0], across).start()
        remote(part, part, h_send.at[n, 1], h_recv.at[n, 1], beside).start()
        return 0

    def pass_on(n, _):
        part = hid.at[d_across, pl.ds(2 * n, 2)]
        drain(part, h_recv.at[n, 0])
        remote(part, part, h_send.at[n, 2], h_recv.at[n, 2], beside).start()
        return 0

    def hidden_of(s):
        return jnp.concatenate([hid[q, s] for q in range(L * C)], axis=1)

    def add_gram(n, _):
        drain(hid.at[d_beside, pl.ds(2 * n, 2)], h_recv.at[n, 1])
        drain(hid.at[d_diag, pl.ds(2 * n, 2)], h_recv.at[n, 2])
        for k in range(2):
            block = hidden_of(2 * n + k)
            system[...] += dot(block, block, NT)
        return 0

    def add_rhs(s, _):
        drain(tfin.at[s], t2_recv.at[s])
        rhs[...] += dot(hidden_of(s), tfin[s])
        return 0

    def turn(step):
        ring_wait(step)
        if step < 3:
            ring_start(step + 1)
        else:
            ring_start_last()
        pack_features(2 * step - 1)
        pack_features(2 * step)
        pack_targets(2 * step - 1, step)
        hop_z(2 * step - 1, step, 2 * step)
        pack_targets(2 * step, Z - step)
        hop_z(2 * step, Z - step, 2 * step - 1)

    turn(1)
    turn(2)
    drain(weights.at[d_across], w_recv.at[0])
    remote(weights.at[d_across], weights.at[d_across], w_send.at[2], w_recv.at[2], beside).start()
    turn(3)
    lax.fori_loop(1, 3, forward, 0)
    drain(weights.at[d_beside], w_recv.at[1])
    drain(weights.at[d_diag], w_recv.at[2])
    lax.fori_loop(0, 2, activate, 0)
    ring_wait_last()
    pack_features(7)
    pack_targets(7, Z // 2)
    activate(2, 0)
    lax.fori_loop(0, 2, pass_on, 0)
    lax.fori_loop(3, 5, forward, 0)
    activate(3, 0)
    pass_on(2, 0)
    drain(tsend.at[0], t1_send.at[5])
    drain(tsend.at[0], t1_send.at[6])
    hop_z(7, Z // 2, 7)
    forward(5, 0)
    pass_on(3, 0)
    forward(6, 0)
    system[...] = jnp.zeros_like(system)
    rhs[...] = jnp.zeros_like(rhs)
    lax.fori_loop(0, 2, add_gram, 0)
    lax.fori_loop(0, 4, add_rhs, 0)
    forward(7, 0)

    def tell(k, _):
        i2, d2 = in_plane(k)
        remote(flags.at[0], flags.at[k], g_send, g_recv, (z * PLANE + i2, d2)).start()
        return 0

    lax.fori_loop(1, PLANE * L * C, tell, 0)
    lax.fori_loop(2, 4, add_gram, 0)
    gram = system[...]
    on_diagonal = lax.broadcasted_iota(jnp.int32, gram.shape, 0) == lax.broadcasted_iota(jnp.int32, gram.shape, 1)
    trace = jnp.sum(jnp.where(on_diagonal, gram, 0.0))
    damping = 0.01 * (trace / keep + 1e-6)
    system[...] = gram + jnp.where(on_diagonal, damping, 0.0)

    lax.fori_loop(4, Z, add_rhs, 0)

    def folded(value):
        rows = value.reshape(value.shape[0] // 8, 8, value.shape[1]).sum(axis=0)
        total = rows[:, 0:128]
        for n in range(1, value.shape[1] // 128):
            total = total + rows[:, n * 128 : (n + 1) * 128]
        return total

    def exchange(it, first, second):
        scal[it, d, 0] = first
        scal[it, d, 1] = second
        copies = []
        for k in range(1, L * C):
            there = (d + k) % (L * C)
            copies.append(
                remote(scal.at[it, d], scal.at[it, d], s_send.at[it, k], s_recv.at[it, k], (e, there))
            )
        for copy in copies:
            copy.start()
        for copy in copies:
            copy.wait()
        sums = scal[it, 0]
        for k in range(1, L * C):
            sums = sums + scal[it, k]
        return jnp.sum(sums[0]), jnp.sum(sums[1])

    rr_old = alpha = None
    for it in range(ITERS):
        residual = rhs[...]
        image = jnp.dot(system[...], residual, precision=lax.Precision.HIGHEST)
        rr, curve = exchange(it, folded(residual * residual), folded(residual * image))
        if it == 0:
            alpha = rr / curve
            vec_p[...] = residual
            vec_s[...] = image
            out_ref[0] = alpha * residual
            rhs[...] = residual - alpha * image
        else:
            beta = rr / rr_old
            alpha = rr / (curve - beta * rr / alpha)
            direction = residual + beta * vec_p[...]
            out_ref[0] += alpha * direction
            if it + 1 < ITERS:
                applied = image + beta * vec_s[...]
                vec_p[...] = direction
                vec_s[...] = applied
                rhs[...] = residual - alpha * applied
        rr_old = rr

    others = flags.at[pl.ds(1, PLANE * L * C - 1)]
    drain(others, g_recv)
    drain(others, g_send)
    flag_ref[...] = jnp.max(flags[...], axis=0)

    drain(tok.at[pl.ds(0, 7)], ring_send)
    drain(idsb.at[pl.ds(0, 7)], idr_send)
    for s in range(Z):
        drain(feats.at[s, pl.ds(0, (PLANE - 1) * CAP)], f_send.at[s])
        drain(tfin.at[s, pl.ds(0, (PLANE * L * C - 1) * CAP)], t2_send.at[s])
    for n in (1, 2, 3, 4, 7):
        drain(tsend.at[0], t1_send.at[n])
    for n in range(3):
        drain(weights.at[0], w_send.at[n])
    for n in range(Z // 2):
        for k in range(3):
            drain(hid.at[0, pl.ds(0, 2)], h_send.at[n, k])


def refit(limits, number, tokens, expert_ids, targets, gate_weight, up_weight, kept_units):
    most, spare = limits
    tok_rows, model_width = tokens.shape
    routes = expert_ids.shape[1]
    keep = kept_units.shape[1]
    rows, units = gate_weight.shape[1:]
    ids = expert_ids.reshape(1, -1)
    targets = targets.reshape(-1, model_width)
    part = L * C
    out_cols = model_width // part
    slots = PLANE * CAP
    vmem = pl.BlockSpec(memory_space=pltpu.VMEM)
    hbm = pl.BlockSpec(memory_space=pl.ANY)
    dma = pltpu.SemaphoreType.DMA
    bf, f32 = jnp.bfloat16, jnp.float32
    return pl.pallas_call(
        functools.partial(kernel, limits),
        out_shape=(jax.ShapeDtypeStruct((1, keep, out_cols), f32), jax.ShapeDtypeStruct((8, 128), f32)),
        in_specs=[vmem, vmem, hbm, hbm, hbm, hbm],
        out_specs=(vmem, vmem),
        scratch_shapes=[
            pltpu.VMEM((Z, tok_rows + spare, model_width), bf),
            pltpu.VMEM((Z, 8, tok_rows * routes), jnp.int32),
            pltpu.VMEM((tok_rows * routes, model_width), bf),
            pltpu.VMEM((rows, units), bf),
            pltpu.VMEM((rows, units), bf),
            pltpu.VMEM((tok_rows * routes, tok_rows * routes), bf),
            pltpu.VMEM((Z, slots, model_width), bf),
            pltpu.VMEM((Z, slots, model_width), bf),
            pltpu.VMEM((part, 2 * keep, rows), bf),
            pltpu.VMEM((part, Z, keep, slots), bf),
            pltpu.VMEM((Z, most, model_width), bf),
            pltpu.VMEM((Z, most, model_width), bf),
            pltpu.VMEM((Z, part, slots, out_cols), bf),
            pltpu.VMEM((Z, part * slots, out_cols), bf),
            pltpu.VMEM((Z, slots, most + spare), bf),
            pltpu.VMEM((keep, out_cols), f32),
            pltpu.VMEM((keep, keep), f32),
            pltpu.VMEM((keep, out_cols), f32),
            pltpu.VMEM((keep, out_cols), f32),
            pltpu.VMEM((ITERS, part, 2, 8, 128), f32),
            pltpu.VMEM((PLANE * part, 8, 128), f32),
            dma((4,)), dma, dma((5, 2)), dma, dma((5, 2)), dma((Z,)), dma((Z,)), dma((Z,)), dma((Z,)),
            dma((Z,)), dma((Z,)), dma((3,)), dma((3,)), dma((Z // 2, 3)), dma((Z // 2, 3)),
            dma((ITERS, part)), dma((ITERS, part)), dma, dma,
        ],
        compiler_params=pltpu.CompilerParams(
            collective_id=number, has_side_effects=True, vmem_limit_bytes=56 * 2**20
        ),
    )(ids, kept_units, tokens, targets, gate_weight[0], up_weight[0])


def body(*args):
    result, flag = refit((80, 32), 0, *args)
    return lax.cond(flag[0, 0] > 0, lambda: refit((PLANE * CAP, 0), 1, *args)[0], lambda: result)


def solution(mesh):
    placed = (
        P(("expert", "dp"), None),
        P(("expert", "dp"), None),
        P(("expert", "dp"), None, None),
        P("expert", "dp", None),
        P("expert", "dp", None),
        P("expert", None),
    )
    return jax.shard_map(
        body, mesh=mesh, in_specs=placed, out_specs=P("expert", None, "dp"), check_vma=False
    )
```

```python
import functools

import jax
import jax.numpy as jnp
from jax import lax
from jax.experimental import pallas as pl
from jax.experimental.pallas import tpu as pltpu
from jax.sharding import PartitionSpec as P

ITERS = 3
Z, Y, H, L, C = 8, 4, 2, 2, 2
PLANE = Y * H
CAP = 16
MESH = pl.DeviceIdType.MESH
NT = (((1,), (1,)), ((), ()))


def dot(a, b, dims=(((1,), (0,)), ((), ()))):
    return lax.dot_general(a, b, dims, preferred_element_type=jnp.float32)


def kernel(
    limits, ids_ref, kept_ref, tokens_hbm, targets_hbm, gate_hbm, up_hbm, out_ref, flag_ref,
    tok, idsb, targ, gate, up, before, fsend, feats, weights, hid, tsend, tmid, tpack, tfin,
    picked, rhs, system, vec_s, vec_q, vec_r, vec_w, vec_n, scal, flags,
    in_sem, ring_send, ring_recv, idr_send, idr_recv, f_send, f_recv, t1_send, t1_recv,
    t2_send, t2_recv, w_send, w_recv, h_send, h_recv, s_send, s_recv, g_send, g_recv,
):
    most, spare = limits
    tokens_here = tokens_hbm.shape[0]
    e = lax.axis_index("expert")
    d = lax.axis_index("dp")
    z, y, h = e // PLANE, (e // H) % Y, e % H
    l, c = d // C, d % C
    here = y * H + h

    def at_z(o):
        return ((z + o) % Z) * PLANE + here, d

    def in_plane(k):
        y2, h2 = (y + k // 8) % Y, (h + (k // 4) % 2) % H
        l2, c2 = (l + (k // 2) % 2) % L, (c + k % 2) % C
        return y2 * H + h2, l2 * C + c2

    def remote(src, dst, send, recv, device):
        return pltpu.make_async_remote_copy(
            src_ref=src, dst_ref=dst, send_sem=send, recv_sem=recv, device_id=device, device_id_type=MESH
        )

    def drain(ref, sem):
        pltpu.make_async_copy(ref, ref, sem).wait()

    loads = [
        pltpu.make_async_copy(src, dst, in_sem.at[n])
        for n, (src, dst) in enumerate(
            [(tokens_hbm, tok.at[0, pl.ds(0, tokens_here)]), (targets_hbm, targ), (gate_hbm, gate), (up_hbm, up)]
        )
    ]
    for load in loads:
        load.start()

    barrier = pltpu.get_barrier_semaphore()

    def greet_z(o, _):
        pl.semaphore_signal(barrier, inc=1, device_id=at_z(o), device_id_type=MESH)
        return 0

    def greet_plane(k, _):
        i2, d2 = in_plane(k)
        pl.semaphore_signal(barrier, inc=1, device_id=(z * PLANE + i2, d2), device_id_type=MESH)
        return 0

    lax.fori_loop(1, Z, greet_z, 0)
    lax.fori_loop(1, PLANE * L * C, greet_plane, 0)

    routes = idsb.shape[2]
    per_token = ids_ref.shape[0]
    place_at = lax.broadcasted_iota(jnp.int32, (tokens_here, routes), 1)
    token_at = lax.broadcasted_iota(jnp.int32, (tokens_here, routes), 0)
    wide = (place_at // per_token == token_at).astype(jnp.float32).astype(jnp.bfloat16)
    every = dot(ids_ref[...].astype(jnp.float32).astype(jnp.bfloat16), wide)
    place_at = lax.broadcasted_iota(jnp.int32, (per_token, routes), 1)
    route_at = lax.broadcasted_iota(jnp.int32, (per_token, routes), 0)
    ids_row = jnp.sum(jnp.where(place_at % per_token == route_at, every, 0.0), axis=0, keepdims=True)
    idsb[0] = jnp.broadcast_to(ids_row, idsb.shape[1:]).astype(jnp.int32)
    row_at = lax.broadcasted_iota(jnp.int32, (routes, routes), 0)
    col_at = lax.broadcasted_iota(jnp.int32, (routes, routes), 1)
    before[...] = (row_at < col_at).astype(jnp.float32).astype(jnp.bfloat16)

    def places(ids, first, count):
        named = (ids == first + lax.broadcasted_iota(jnp.int32, (count, routes), 0)).astype(jnp.float32)
        rank = dot(named.astype(jnp.bfloat16), before[...])
        return jnp.where(named > 0, rank, -1.0)

    def one_hot(place):
        wide = jnp.broadcast_to(place[:, None, :], (PLANE, CAP, routes))
        slot = lax.broadcasted_iota(jnp.int32, (PLANE, CAP, routes), 1).astype(jnp.float32)
        return (wide == slot).astype(jnp.float32).reshape(PLANE * CAP, routes).astype(jnp.bfloat16)

    def plane_rows(ids):
        plane = ids // PLANE
        named = (plane == lax.broadcasted_iota(jnp.int32, (Z, routes), 0)).astype(jnp.float32)
        rank = dot(named.astype(jnp.bfloat16), before[...])
        rank = jnp.broadcast_to(jnp.sum(named * rank, axis=0, keepdims=True), (Z, routes))
        over = (rank >= most).astype(jnp.float32)
        late = dot(over.astype(jnp.bfloat16), before[...])
        return plane, jnp.where(over > 0, most + late, rank), jnp.sum(over[0:1])

    def row_hot(place, first, count):
        row = first + lax.broadcasted_iota(jnp.int32, (count, routes), 0).astype(jnp.float32)
        return (jnp.broadcast_to(place[0:1], (count, routes)) == row).astype(jnp.float32).astype(jnp.bfloat16)

    my_plane, my_row, _ = plane_rows(idsb[0])
    flags[0] = jnp.zeros_like(flags[0])
    loads[1].wait()
    if spare:
        late_rows = pl.ds(tokens_here, spare)
        tok[0, late_rows] = dot(row_hot(my_row, float(most), spare), targ[...]).astype(jnp.bfloat16)

    pl.semaphore_wait(barrier, Z - 1 + PLANE * L * C - 1)
    loads[0].wait()

    half = tok.shape[1] // 2

    def ring_start(step):
        src_r, src_l = 2 * (step - 1), jnp.maximum(2 * step - 3, 0)
        remote(tok.at[src_r], tok.at[2 * step], ring_send, ring_recv.at[step, 0], at_z(1)).start()
        remote(tok.at[src_l], tok.at[2 * step - 1], ring_send, ring_recv.at[step, 1], at_z(Z - 1)).start()
        remote(idsb.at[src_r], idsb.at[2 * step], idr_send, idr_recv.at[step, 0], at_z(1)).start()
        remote(idsb.at[src_l], idsb.at[2 * step - 1], idr_send, idr_recv.at[step, 1], at_z(Z - 1)).start()

    def ring_wait(step):
        drain(tok.at[2 * step], ring_recv.at[step, 0])
        drain(tok.at[2 * step - 1], ring_recv.at[step, 1])
        drain(idsb.at[2 * step], idr_recv.at[step, 0])
        drain(idsb.at[2 * step - 1], idr_recv.at[step, 1])

    low, high = pl.ds(0, half), pl.ds(half, half)

    def ring_start_last():
        remote(tok.at[6, low], tok.at[7, low], ring_send, ring_recv.at[4, 0], at_z(1)).start()
        remote(tok.at[5, high], tok.at[7, high], ring_send, ring_recv.at[4, 1], at_z(Z - 1)).start()
        remote(idsb.at[6], idsb.at[7], idr_send, idr_recv.at[4, 0], at_z(1)).start()

    def ring_wait_last():
        drain(tok.at[7, low], ring_recv.at[4, 0])
        drain(tok.at[7, high], ring_recv.at[4, 1])
        drain(idsb.at[7], idr_recv.at[4, 0])

    def pack_features(s):
        place = places(idsb[s], z * PLANE, PLANE)
        hot = one_hot(place)
        tokens_of = (
            lax.broadcasted_iota(jnp.int32, (routes, tokens_here), 0) // (routes // tokens_here)
            == lax.broadcasted_iota(jnp.int32, (routes, tokens_here), 1)
        ).astype(jnp.float32).astype(jnp.bfloat16)
        picks = dot(hot, tokens_of).astype(jnp.bfloat16)
        fsend[s] = dot(picks, tok[s, pl.ds(0, tokens_here)]).astype(jnp.bfloat16)

        def push(k, _):
            y2, h2 = (y + k // 2) % Y, (h + k % 2) % H
            d2 = ((l + k % 2) % L) * C + c
            i2 = y2 * H + h2
            rows = pl.ds(pl.multiple_of(i2 * CAP, CAP), CAP)
            mine = pl.ds(pl.multiple_of(here * CAP, CAP), CAP)
            remote(
                fsend.at[s, rows], feats.at[s, mine], f_send.at[s], f_recv.at[s], (z * PLANE + i2, d2)
            ).start()
            return 0

        lax.fori_loop(1, PLANE, push, 0)
        mine = pl.ds(pl.multiple_of(here * CAP, CAP), CAP)
        pltpu.make_async_copy(fsend.at[s, mine], feats.at[s, mine], f_recv.at[s]).start()
        plane, row, late = plane_rows(idsb[s])
        picked[s] = dot(hot, row_hot(jnp.where(plane == z, row, -1.0), 0.0, most + spare), NT).astype(jnp.bfloat16)
        flags[0] = jnp.maximum(flags[0], late - float(spare))
        return hot

    def pack_targets(s, o):
        place = jnp.where(my_plane == (z + o) % Z, my_row, -1.0)
        tsend[s] = dot(row_hot(place, 0.0, most), targ[...]).astype(jnp.bfloat16)

    def hop_z(s, o, other):
        remote(tsend.at[s], tmid.at[other], t1_send.at[s], t1_recv.at[other], at_z(o)).start()

    def spread(s, packed):
        width = tpack.shape[3]
        for n in range(L * C):
            tpack[s, n] = packed[:, n * width : (n + 1) * width].astype(jnp.bfloat16)

        def push(k, _):
            i2, d2 = in_plane(k)
            owner = ((l + (k // 4) % 2) % L) * C + c
            rows = pl.ds(pl.multiple_of(i2 * CAP, CAP), CAP)
            there = pl.ds(pl.multiple_of((owner * PLANE + here) * CAP, CAP), CAP)
            remote(
                tpack.at[s, d2, rows], tfin.at[s, there], t2_send.at[s], t2_recv.at[s], (z * PLANE + i2, d2)
            ).start()
            return 0

        lax.fori_loop(1, PLANE * L * C, push, 0)
        rows = pl.ds(pl.multiple_of(here * CAP, CAP), CAP)
        there = pl.ds(pl.multiple_of((d * PLANE + here) * CAP, CAP), CAP)
        pltpu.make_async_copy(tpack.at[s, d, rows], tfin.at[s, there], t2_recv.at[s]).start()

    across = (e, ((l + 1) % L) * C + c)
    beside = (e, l * C + (c + 1) % C)
    d_across = ((l + 1) % L) * C + c
    d_beside = l * C + (c + 1) % C
    d_diag = ((l + 1) % L) * C + (c + 1) % C

    ring_start(1)
    spread(0, dot(pack_features(0), targ[...]))

    loads[2].wait()
    loads[3].wait()
    keep = kept_ref.shape[1]
    hidden_units = gate.shape[1]
    kept_down = jnp.transpose(jnp.broadcast_to(kept_ref[...].astype(jnp.float32), (128, keep)))
    lane = lax.broadcasted_iota(jnp.int32, (keep, 128), 1).astype(jnp.float32)
    chosen = jnp.concatenate(
        [(kept_down == lane + float(128 * n)).astype(jnp.float32) for n in range(hidden_units // 128)], axis=1
    ).astype(jnp.bfloat16)
    weights[d, pl.ds(0, keep)] = dot(chosen, gate[...], NT).astype(jnp.bfloat16)
    weights[d, pl.ds(keep, keep)] = dot(chosen, up[...], NT).astype(jnp.bfloat16)
    remote(weights.at[d], weights.at[d], w_send.at[0], w_recv.at[0], across).start()
    remote(weights.at[d], weights.at[d], w_send.at[1], w_recv.at[1], beside).start()

    def forward(s, _):
        drain(tmid.at[s], t1_recv.at[s])
        rows = tmid[s]
        if spare:
            rows = jnp.concatenate([rows, tok[s, late_rows]], axis=0)
        spread(s, dot(picked[s], rows))
        return 0

    def activate(n, _):
        drain(feats.at[2 * n], f_recv.at[2 * n])
        drain(feats.at[2 * n + 1], f_recv.at[2 * n + 1])
        rows = feats.shape[1]
        block = feats[pl.ds(2 * n, 2)].reshape(2 * rows, feats.shape[2])
        width = weights.shape[2]
        acts = dot(weights[0], block[:, 0:width], NT)
        for q in range(1, L * C):
            acts = acts + dot(weights[q], block[:, q * width : (q + 1) * width], NT)
        gate_acts, up_acts = acts[:keep], acts[keep:]
        hidden = (gate_acts / (1.0 + jnp.exp(-gate_acts)) * up_acts).astype(jnp.bfloat16)
        hid[d, 2 * n] = hidden[:, :rows]
        hid[d, 2 * n + 1] = hidden[:, rows:]
        part = hid.at[d, pl.ds(2 * n, 2)]
        remote(part, part, h_send.at[n, 0], h_recv.at[n, 0], across).start()
        remote(part, part, h_send.at[n, 1], h_recv.at[n, 1], beside).start()
        return 0

    def pass_on(n, _):
        part = hid.at[d_across, pl.ds(2 * n, 2)]
        drain(part, h_recv.at[n, 0])
        remote(part, part, h_send.at[n, 2], h_recv.at[n, 2], beside).start()
        return 0

    def hidden_of(s):
        return jnp.concatenate([hid[q, s] for q in range(L * C)], axis=1)

    def add_gram(n, _):
        drain(hid.at[d_beside, pl.ds(2 * n, 2)], h_recv.at[n, 1])
        drain(hid.at[d_diag, pl.ds(2 * n, 2)], h_recv.at[n, 2])
        for k in range(2):
            block = hidden_of(2 * n + k)
            system[...] += dot(block, block, NT)
        return 0

    def add_rhs(s, _):
        drain(tfin.at[s], t2_recv.at[s])
        rhs[...] += dot(hidden_of(s), tfin[s])
        return 0

    def turn(step):
        ring_wait(step)
        if step < 3:
            ring_start(step + 1)
        else:
            ring_start_last()
        pack_features(2 * step - 1)
        pack_features(2 * step)
        pack_targets(2 * step - 1, step)
        hop_z(2 * step - 1, step, 2 * step)
        pack_targets(2 * step, Z - step)
        hop_z(2 * step, Z - step, 2 * step - 1)

    turn(1)
    turn(2)
    drain(weights.at[d_across], w_recv.at[0])
    remote(weights.at[d_across], weights.at[d_across], w_send.at[2], w_recv.at[2], beside).start()
    turn(3)
    lax.fori_loop(1, 3, forward, 0)
    drain(weights.at[d_beside], w_recv.at[1])
    drain(weights.at[d_diag], w_recv.at[2])
    lax.fori_loop(0, 2, activate, 0)
    ring_wait_last()
    pack_features(7)
    pack_targets(7, Z // 2)
    def tell(k, _):
        i2, d2 = in_plane(k)
        remote(flags.at[0], flags.at[k], g_send, g_recv, (z * PLANE + i2, d2)).start()
        return 0

    lax.fori_loop(1, PLANE * L * C, tell, 0)
    activate(2, 0)
    lax.fori_loop(0, 2, pass_on, 0)
    lax.fori_loop(3, 5, forward, 0)
    activate(3, 0)
    pass_on(2, 0)
    drain(tsend.at[0], t1_send.at[5])
    drain(tsend.at[0], t1_send.at[6])
    hop_z(7, Z // 2, 7)
    forward(5, 0)
    pass_on(3, 0)
    forward(6, 0)
    system[...] = jnp.zeros_like(system)
    rhs[...] = jnp.zeros_like(rhs)
    lax.fori_loop(0, 2, add_gram, 0)
    lax.fori_loop(0, 4, add_rhs, 0)
    forward(7, 0)

    lax.fori_loop(2, 4, add_gram, 0)
    gram = system[...]
    on_diagonal = lax.broadcasted_iota(jnp.int32, gram.shape, 0) == lax.broadcasted_iota(jnp.int32, gram.shape, 1)
    trace = jnp.sum(jnp.where(on_diagonal, gram, 0.0))
    damping = 0.01 * (trace / keep + 1e-6)
    system[...] = gram + jnp.where(on_diagonal, damping, 0.0)

    lax.fori_loop(4, Z, add_rhs, 0)

    def folded(value):
        rows = value.reshape(value.shape[0] // 8, 8, value.shape[1]).sum(axis=0)
        total = rows[:, 0:128]
        for n in range(1, value.shape[1] // 128):
            total = total + rows[:, n * 128 : (n + 1) * 128]
        return total

    def times_system(ref):
        return jnp.dot(system[...], ref[...], precision=lax.Precision.HIGHEST)

    def share(it, residual, image):
        scal[it, d, 0] = folded(residual * residual)
        scal[it, d, 1] = folded(residual * image)
        copies = []
        for k in range(1, L * C):
            there = (d + k) % (L * C)
            copies.append(
                remote(scal.at[it, d], scal.at[it, d], s_send.at[it, k], s_recv.at[it, k], (e, there))
            )
        for copy in copies:
            copy.start()
        return copies

    def collect(it, copies):
        for copy in copies:
            copy.wait()
        sums = scal[it, 0]
        for k in range(1, L * C):
            sums = sums + scal[it, k]
        return jnp.sum(sums[0]), jnp.sum(sums[1])

    vec_s[...] = times_system(rhs)
    copies = share(0, rhs[...], vec_s[...])
    vec_q[...] = times_system(vec_s)
    rr0, curve = collect(0, copies)
    alpha0 = rr0 / curve
    vec_r[...] = rhs[...] - alpha0 * vec_s[...]
    vec_w[...] = vec_s[...] - alpha0 * vec_q[...]
    copies = share(1, vec_r[...], vec_w[...])
    vec_n[...] = times_system(vec_w)
    rr1, curve = collect(1, copies)
    beta1 = rr1 / rr0
    alpha1 = rr1 / (curve - beta1 * rr1 / alpha0)
    last = vec_r[...] - alpha1 * (vec_w[...] + beta1 * vec_s[...])
    copies = share(2, last, vec_w[...] - alpha1 * (vec_n[...] + beta1 * vec_q[...]))
    vec_n[...] = last
    rr2, curve = collect(2, copies)
    beta2 = rr2 / rr1
    alpha2 = rr2 / (curve - beta2 * rr2 / alpha1)
    of_r1 = alpha1 + alpha2 * beta2
    of_r0 = alpha0 + of_r1 * beta1
    out_ref[0] = of_r0 * rhs[...] + of_r1 * vec_r[...] + alpha2 * vec_n[...]

    others = flags.at[pl.ds(1, PLANE * L * C - 1)]
    drain(others, g_recv)
    drain(others, g_send)
    flag_ref[0, 0] = (jnp.max(flags[...]) > 0).astype(jnp.int32)

    drain(tok.at[pl.ds(0, 7)], ring_send)
    drain(idsb.at[pl.ds(0, 7)], idr_send)
    for s in range(Z):
        drain(feats.at[s, pl.ds(0, (PLANE - 1) * CAP)], f_send.at[s])
        drain(tfin.at[s, pl.ds(0, (PLANE * L * C - 1) * CAP)], t2_send.at[s])
    for n in (1, 2, 3, 4, 7):
        drain(tsend.at[0], t1_send.at[n])
    for n in range(3):
        drain(weights.at[0], w_send.at[n])
    for n in range(Z // 2):
        for k in range(3):
            drain(hid.at[0, pl.ds(0, 2)], h_send.at[n, k])


def refit(limits, number, tokens, expert_ids, targets, gate_weight, up_weight, kept_units):
    most, spare = limits
    tok_rows, model_width = tokens.shape
    routes = expert_ids.shape[1]
    keep = kept_units.shape[1]
    rows, units = gate_weight.shape[1:]
    ids = expert_ids.T
    targets = targets.reshape(-1, model_width)
    part = L * C
    out_cols = model_width // part
    slots = PLANE * CAP
    vmem = pl.BlockSpec(memory_space=pltpu.VMEM)
    hbm = pl.BlockSpec(memory_space=pl.ANY)
    dma = pltpu.SemaphoreType.DMA
    bf, f32 = jnp.bfloat16, jnp.float32
    return pl.pallas_call(
        functools.partial(kernel, limits),
        out_shape=(jax.ShapeDtypeStruct((1, keep, out_cols), f32), jax.ShapeDtypeStruct((1, 1), jnp.int32)),
        in_specs=[vmem, vmem, hbm, hbm, hbm, hbm],
        out_specs=(vmem, pl.BlockSpec(memory_space=pltpu.SMEM)),
        scratch_shapes=[
            pltpu.VMEM((Z, tok_rows + spare, model_width), bf),
            pltpu.VMEM((Z, 8, tok_rows * routes), jnp.int32),
            pltpu.VMEM((tok_rows * routes, model_width), bf),
            pltpu.VMEM((rows, units), bf),
            pltpu.VMEM((rows, units), bf),
            pltpu.VMEM((tok_rows * routes, tok_rows * routes), bf),
            pltpu.VMEM((Z, slots, model_width), bf),
            pltpu.VMEM((Z, slots, model_width), bf),
            pltpu.VMEM((part, 2 * keep, rows), bf),
            pltpu.VMEM((part, Z, keep, slots), bf),
            pltpu.VMEM((Z, most, model_width), bf),
            pltpu.VMEM((Z, most, model_width), bf),
            pltpu.VMEM((Z, part, slots, out_cols), bf),
            pltpu.VMEM((Z, part * slots, out_cols), bf),
            pltpu.VMEM((Z, slots, most + spare), bf),
            pltpu.VMEM((keep, out_cols), f32),
            pltpu.VMEM((keep, keep), f32),
            pltpu.VMEM((keep, out_cols), f32),
            pltpu.VMEM((keep, out_cols), f32),
            pltpu.VMEM((keep, out_cols), f32),
            pltpu.VMEM((keep, out_cols), f32),
            pltpu.VMEM((keep, out_cols), f32),
            pltpu.VMEM((ITERS, part, 2, 8, 128), f32),
            pltpu.VMEM((PLANE * part, 8, 128), f32),
            dma((4,)), dma, dma((5, 2)), dma, dma((5, 2)), dma((Z,)), dma((Z,)), dma((Z,)), dma((Z,)),
            dma((Z,)), dma((Z,)), dma((3,)), dma((3,)), dma((Z // 2, 3)), dma((Z // 2, 3)),
            dma((ITERS, part)), dma((ITERS, part)), dma, dma,
        ],
        compiler_params=pltpu.CompilerParams(
            collective_id=number, has_side_effects=True, vmem_limit_bytes=56 * 2**20
        ),
    )(ids, kept_units, tokens, targets, gate_weight[0], up_weight[0])


def body(*args):
    result, flag = refit((80, 32), 0, *args)
    return lax.cond(flag[0, 0] > 0, lambda: refit((PLANE * CAP, 0), 1, *args)[0], lambda: result)


def solution(mesh):
    placed = (
        P(("expert", "dp"), None),
        P(("expert", "dp"), None),
        P(("expert", "dp"), None, None),
        P("expert", "dp", None),
        P("expert", "dp", None),
        P("expert", None),
    )
    return jax.shard_map(
        body, mesh=mesh, in_specs=placed, out_specs=P("expert", None, "dp"), check_vma=False
    )
```

```python
import functools

import jax
import jax.numpy as jnp
from jax import lax
from jax.experimental import pallas as pl
from jax.experimental.pallas import tpu as pltpu
from jax.sharding import PartitionSpec as P

ITERS = 3
Z, Y, H, L, C = 8, 4, 2, 2, 2
PLANE = Y * H
CAP = 16
MESH = pl.DeviceIdType.MESH
NT = (((1,), (1,)), ((), ()))


def dot(a, b, dims=(((1,), (0,)), ((), ()))):
    return lax.dot_general(a, b, dims, preferred_element_type=jnp.float32)


def kernel(
    limits, ids_ref, kept_ref, tokens_hbm, targets_hbm, gate_hbm, up_hbm, out_ref, flag_ref,
    tok, idsb, targ, gate, up, before, fsend, feats, weights, hid, tsend, tmid, tpack, tfin,
    picked, rhs, system, vec_s, vec_q, vec_r, vec_w, vec_n, scal, flags,
    in_sem, ring_send, ring_recv, idr_send, idr_recv, f_send, f_recv, t1_send, t1_recv,
    t2_send, t2_recv, w_send, w_recv, h_send, h_recv, s_send, s_recv, g_send, g_recv, v_send, v_recv,
):
    most, spare = limits
    tokens_here = tokens_hbm.shape[0]
    e = lax.axis_index("expert")
    d = lax.axis_index("dp")
    z, y, h = e // PLANE, (e // H) % Y, e % H
    l, c = d // C, d % C
    here = y * H + h

    def at_z(o):
        return ((z + o) % Z) * PLANE + here, d

    def in_plane(k):
        y2, h2 = (y + k // 8) % Y, (h + (k // 4) % 2) % H
        l2, c2 = (l + (k // 2) % 2) % L, (c + k % 2) % C
        return y2 * H + h2, l2 * C + c2

    def remote(src, dst, send, recv, device):
        return pltpu.make_async_remote_copy(
            src_ref=src, dst_ref=dst, send_sem=send, recv_sem=recv, device_id=device, device_id_type=MESH
        )

    def drain(ref, sem):
        pltpu.make_async_copy(ref, ref, sem).wait()

    loads = [
        pltpu.make_async_copy(src, dst, in_sem.at[n])
        for n, (src, dst) in enumerate(
            [(tokens_hbm, tok.at[0, pl.ds(0, tokens_here)]), (targets_hbm, targ), (gate_hbm, gate), (up_hbm, up)]
        )
    ]
    for load in loads:
        load.start()

    barrier = pltpu.get_barrier_semaphore()

    def greet_z(o, _):
        pl.semaphore_signal(barrier, inc=1, device_id=at_z(o), device_id_type=MESH)
        return 0

    def greet_plane(k, _):
        i2, d2 = in_plane(k)
        pl.semaphore_signal(barrier, inc=1, device_id=(z * PLANE + i2, d2), device_id_type=MESH)
        return 0

    lax.fori_loop(1, Z, greet_z, 0)
    lax.fori_loop(1, PLANE * L * C, greet_plane, 0)

    routes = idsb.shape[2]
    per_token = ids_ref.shape[0]
    place_at = lax.broadcasted_iota(jnp.int32, (tokens_here, routes), 1)
    token_at = lax.broadcasted_iota(jnp.int32, (tokens_here, routes), 0)
    wide = (place_at // per_token == token_at).astype(jnp.float32).astype(jnp.bfloat16)
    every = dot(ids_ref[...].astype(jnp.float32).astype(jnp.bfloat16), wide)
    place_at = lax.broadcasted_iota(jnp.int32, (per_token, routes), 1)
    route_at = lax.broadcasted_iota(jnp.int32, (per_token, routes), 0)
    ids_row = jnp.sum(jnp.where(place_at % per_token == route_at, every, 0.0), axis=0, keepdims=True)
    idsb[0] = jnp.broadcast_to(ids_row, idsb.shape[1:]).astype(jnp.int32)

    pl.semaphore_wait(barrier, Z - 1 + PLANE * L * C - 1)
    loads[0].wait()

    def pass_rows(first, count, step, send, recv):
        if step < 4:
            rows = pl.ds(first, count)
            src_r, src_l = 2 * (step - 1), max(2 * step - 3, 0)
            remote(tok.at[src_r, rows], tok.at[2 * step, rows], send, recv.at[step, 0], at_z(1)).start()
            remote(tok.at[src_l, rows], tok.at[2 * step - 1, rows], send, recv.at[step, 1], at_z(Z - 1)).start()
        else:
            low, high = pl.ds(first, count // 2), pl.ds(first + count // 2, count // 2)
            remote(tok.at[6, low], tok.at[7, low], send, recv.at[4, 0], at_z(1)).start()
            remote(tok.at[5, high], tok.at[7, high], send, recv.at[4, 1], at_z(Z - 1)).start()

    def take_rows(first, count, step, recv):
        half = count // 2
        of_r = tok.at[2 * step, pl.ds(first, count)] if step < 4 else tok.at[7, pl.ds(first, half)]
        of_l = tok.at[2 * step - 1, pl.ds(first, count)] if step < 4 else tok.at[7, pl.ds(first + half, half)]
        drain(of_r, recv.at[step, 0])
        drain(of_l, recv.at[step, 1])

    def ring_start(step):
        pass_rows(0, tokens_here, step, ring_send, ring_recv)
        src_r, src_l = 2 * (step - 1), max(2 * step - 3, 0)
        to_r = 2 * step if step < 4 else 7
        remote(idsb.at[src_r], idsb.at[to_r], idr_send, idr_recv.at[step, 0], at_z(1)).start()
        if step < 4:
            remote(idsb.at[src_l], idsb.at[2 * step - 1], idr_send, idr_recv.at[step, 1], at_z(Z - 1)).start()

    def ring_wait(step):
        take_rows(0, tokens_here, step, ring_recv)
        drain(idsb.at[2 * step if step < 4 else 7], idr_recv.at[step, 0])
        if step < 4:
            drain(idsb.at[2 * step - 1], idr_recv.at[step, 1])

    def spare_start(step):
        if spare:
            pass_rows(tokens_here, spare, step, v_send, v_recv)

    def spare_wait(step):
        if spare:
            take_rows(tokens_here, spare, step, v_recv)

    ring_start(1)
    row_at = lax.broadcasted_iota(jnp.int32, (routes, routes), 0)
    col_at = lax.broadcasted_iota(jnp.int32, (routes, routes), 1)
    before[...] = (row_at < col_at).astype(jnp.float32).astype(jnp.bfloat16)

    def places(ids, first, count):
        named = (ids == first + lax.broadcasted_iota(jnp.int32, (count, routes), 0)).astype(jnp.float32)
        rank = dot(named.astype(jnp.bfloat16), before[...])
        return jnp.where(named > 0, rank, -1.0)

    def one_hot(place):
        wide = jnp.broadcast_to(place[:, None, :], (PLANE, CAP, routes))
        slot = lax.broadcasted_iota(jnp.int32, (PLANE, CAP, routes), 1).astype(jnp.float32)
        return (wide == slot).astype(jnp.float32).reshape(PLANE * CAP, routes).astype(jnp.bfloat16)

    def plane_rows(ids):
        plane = ids // PLANE
        named = (plane == lax.broadcasted_iota(jnp.int32, (Z, routes), 0)).astype(jnp.float32)
        rank = dot(named.astype(jnp.bfloat16), before[...])
        rank = jnp.broadcast_to(jnp.sum(named * rank, axis=0, keepdims=True), (Z, routes))
        over = (rank >= most).astype(jnp.float32)
        late = dot(over.astype(jnp.bfloat16), before[...])
        return plane, jnp.where(over > 0, most + late, rank), jnp.sum(over[0:1])

    def row_hot(place, first, count):
        row = first + lax.broadcasted_iota(jnp.int32, (count, routes), 0).astype(jnp.float32)
        return (jnp.broadcast_to(place[0:1], (count, routes)) == row).astype(jnp.float32).astype(jnp.bfloat16)

    my_plane, my_row, _ = plane_rows(idsb[0])
    flags[0] = jnp.zeros_like(flags[0])
    loads[1].wait()
    if spare:
        late_rows = pl.ds(tokens_here, spare)
        tok[0, late_rows] = dot(row_hot(my_row, float(most), spare), targ[...]).astype(jnp.bfloat16)
        spare_start(1)

    def pack_features(s):
        place = places(idsb[s], z * PLANE, PLANE)
        hot = one_hot(place)
        tokens_of = (
            lax.broadcasted_iota(jnp.int32, (routes, tokens_here), 0) // (routes // tokens_here)
            == lax.broadcasted_iota(jnp.int32, (routes, tokens_here), 1)
        ).astype(jnp.float32).astype(jnp.bfloat16)
        picks = dot(hot, tokens_of).astype(jnp.bfloat16)
        fsend[s] = dot(picks, tok[s, pl.ds(0, tokens_here)]).astype(jnp.bfloat16)

        def push(k, _):
            y2, h2 = (y + k // 2) % Y, (h + k % 2) % H
            d2 = ((l + k % 2) % L) * C + c
            i2 = y2 * H + h2
            rows = pl.ds(pl.multiple_of(i2 * CAP, CAP), CAP)
            mine = pl.ds(pl.multiple_of(here * CAP, CAP), CAP)
            remote(
                fsend.at[s, rows], feats.at[s, mine], f_send.at[s], f_recv.at[s], (z * PLANE + i2, d2)
            ).start()
            return 0

        lax.fori_loop(1, PLANE, push, 0)
        mine = pl.ds(pl.multiple_of(here * CAP, CAP), CAP)
        pltpu.make_async_copy(fsend.at[s, mine], feats.at[s, mine], f_recv.at[s]).start()
        plane, row, late = plane_rows(idsb[s])
        picked[s] = dot(hot, row_hot(jnp.where(plane == z, row, -1.0), 0.0, most + spare), NT).astype(jnp.bfloat16)
        flags[0] = jnp.maximum(flags[0], late - float(spare))
        return hot

    def pack_targets(s, o):
        place = jnp.where(my_plane == (z + o) % Z, my_row, -1.0)
        tsend[s] = dot(row_hot(place, 0.0, most), targ[...]).astype(jnp.bfloat16)

    def hop_z(s, o, other):
        remote(tsend.at[s], tmid.at[other], t1_send.at[s], t1_recv.at[other], at_z(o)).start()

    def spread(s, packed):
        width = tpack.shape[3]
        for n in range(L * C):
            tpack[s, n] = packed[:, n * width : (n + 1) * width].astype(jnp.bfloat16)

        def push(k, _):
            i2, d2 = in_plane(k)
            owner = ((l + (k // 4) % 2) % L) * C + c
            rows = pl.ds(pl.multiple_of(i2 * CAP, CAP), CAP)
            there = pl.ds(pl.multiple_of((owner * PLANE + here) * CAP, CAP), CAP)
            remote(
                tpack.at[s, d2, rows], tfin.at[s, there], t2_send.at[s], t2_recv.at[s], (z * PLANE + i2, d2)
            ).start()
            return 0

        lax.fori_loop(1, PLANE * L * C, push, 0)
        rows = pl.ds(pl.multiple_of(here * CAP, CAP), CAP)
        there = pl.ds(pl.multiple_of((d * PLANE + here) * CAP, CAP), CAP)
        pltpu.make_async_copy(tpack.at[s, d, rows], tfin.at[s, there], t2_recv.at[s]).start()

    across = (e, ((l + 1) % L) * C + c)
    beside = (e, l * C + (c + 1) % C)
    d_across = ((l + 1) % L) * C + c
    d_beside = l * C + (c + 1) % C
    d_diag = ((l + 1) % L) * C + (c + 1) % C

    spread(0, dot(pack_features(0), targ[...]))

    loads[2].wait()
    loads[3].wait()
    keep = kept_ref.shape[1]
    hidden_units = gate.shape[1]
    kept_down = jnp.transpose(jnp.broadcast_to(kept_ref[...].astype(jnp.float32), (128, keep)))
    lane = lax.broadcasted_iota(jnp.int32, (keep, 128), 1).astype(jnp.float32)
    chosen = jnp.concatenate(
        [(kept_down == lane + float(128 * n)).astype(jnp.float32) for n in range(hidden_units // 128)], axis=1
    ).astype(jnp.bfloat16)
    weights[d, pl.ds(0, keep)] = dot(chosen, gate[...], NT).astype(jnp.bfloat16)
    weights[d, pl.ds(keep, keep)] = dot(chosen, up[...], NT).astype(jnp.bfloat16)
    remote(weights.at[d], weights.at[d], w_send.at[0], w_recv.at[0], across).start()
    remote(weights.at[d], weights.at[d], w_send.at[1], w_recv.at[1], beside).start()

    def forward(s, _):
        drain(tmid.at[s], t1_recv.at[s])
        rows = tmid[s]
        if spare:
            rows = jnp.concatenate([rows, tok[s, late_rows]], axis=0)
        spread(s, dot(picked[s], rows))
        return 0

    def activate(n, _):
        drain(feats.at[2 * n], f_recv.at[2 * n])
        drain(feats.at[2 * n + 1], f_recv.at[2 * n + 1])
        rows = feats.shape[1]
        block = feats[pl.ds(2 * n, 2)].reshape(2 * rows, feats.shape[2])
        width = weights.shape[2]
        acts = dot(weights[0], block[:, 0:width], NT)
        for q in range(1, L * C):
            acts = acts + dot(weights[q], block[:, q * width : (q + 1) * width], NT)
        gate_acts, up_acts = acts[:keep], acts[keep:]
        hidden = (gate_acts / (1.0 + jnp.exp(-gate_acts)) * up_acts).astype(jnp.bfloat16)
        hid[d, 2 * n] = hidden[:, :rows]
        hid[d, 2 * n + 1] = hidden[:, rows:]
        part = hid.at[d, pl.ds(2 * n, 2)]
        remote(part, part, h_send.at[n, 0], h_recv.at[n, 0], across).start()
        remote(part, part, h_send.at[n, 1], h_recv.at[n, 1], beside).start()
        return 0

    def pass_on(n, _):
        part = hid.at[d_across, pl.ds(2 * n, 2)]
        drain(part, h_recv.at[n, 0])
        remote(part, part, h_send.at[n, 2], h_recv.at[n, 2], beside).start()
        return 0

    def hidden_of(s):
        return jnp.concatenate([hid[q, s] for q in range(L * C)], axis=1)

    def add_gram(n, _):
        drain(hid.at[d_beside, pl.ds(2 * n, 2)], h_recv.at[n, 1])
        drain(hid.at[d_diag, pl.ds(2 * n, 2)], h_recv.at[n, 2])
        for k in range(2):
            block = hidden_of(2 * n + k)
            system[...] += dot(block, block, NT)
        return 0

    def add_rhs(s, _):
        drain(tfin.at[s], t2_recv.at[s])
        rhs[...] += dot(hidden_of(s), tfin[s])
        return 0

    def turn(step):
        ring_wait(step)
        ring_start(step + 1)
        pack_features(2 * step - 1)
        pack_features(2 * step)
        spare_wait(step)
        spare_start(step + 1)
        pack_targets(2 * step - 1, step)
        hop_z(2 * step - 1, step, 2 * step)
        pack_targets(2 * step, Z - step)
        hop_z(2 * step, Z - step, 2 * step - 1)

    turn(1)
    turn(2)
    drain(weights.at[d_across], w_recv.at[0])
    remote(weights.at[d_across], weights.at[d_across], w_send.at[2], w_recv.at[2], beside).start()
    turn(3)
    lax.fori_loop(1, 3, forward, 0)
    drain(weights.at[d_beside], w_recv.at[1])
    drain(weights.at[d_diag], w_recv.at[2])
    lax.fori_loop(0, 2, activate, 0)
    ring_wait(4)
    pack_features(7)
    pack_targets(7, Z // 2)
    def tell(k, _):
        i2, d2 = in_plane(k)
        remote(flags.at[0], flags.at[k], g_send, g_recv, (z * PLANE + i2, d2)).start()
        return 0

    lax.fori_loop(1, PLANE * L * C, tell, 0)
    activate(2, 0)
    lax.fori_loop(0, 2, pass_on, 0)
    lax.fori_loop(3, 5, forward, 0)
    activate(3, 0)
    pass_on(2, 0)
    drain(tsend.at[0], t1_send.at[5])
    drain(tsend.at[0], t1_send.at[6])
    hop_z(7, Z // 2, 7)
    forward(5, 0)
    pass_on(3, 0)
    forward(6, 0)
    system[...] = jnp.zeros_like(system)
    rhs[...] = jnp.zeros_like(rhs)
    lax.fori_loop(0, 2, add_gram, 0)
    lax.fori_loop(0, 4, add_rhs, 0)
    spare_wait(4)
    forward(7, 0)

    lax.fori_loop(2, 4, add_gram, 0)
    gram = system[...]
    on_diagonal = lax.broadcasted_iota(jnp.int32, gram.shape, 0) == lax.broadcasted_iota(jnp.int32, gram.shape, 1)
    trace = jnp.sum(jnp.where(on_diagonal, gram, 0.0))
    damping = 0.01 * (trace / keep + 1e-6)
    system[...] = gram + jnp.where(on_diagonal, damping, 0.0)

    lax.fori_loop(4, Z, add_rhs, 0)

    def folded(value):
        rows = value.reshape(value.shape[0] // 8, 8, value.shape[1]).sum(axis=0)
        total = rows[:, 0:128]
        for n in range(1, value.shape[1] // 128):
            total = total + rows[:, n * 128 : (n + 1) * 128]
        return total

    def times_system(ref):
        return jnp.dot(system[...], ref[...], precision=lax.Precision.HIGHEST)

    def share(it, residual, image):
        scal[it, d, 0] = folded(residual * residual)
        scal[it, d, 1] = folded(residual * image)
        copies = []
        for k in range(1, L * C):
            there = (d + k) % (L * C)
            copies.append(
                remote(scal.at[it, d], scal.at[it, d], s_send.at[it, k], s_recv.at[it, k], (e, there))
            )
        for copy in copies:
            copy.start()
        return copies

    def collect(it, copies):
        for copy in copies:
            copy.wait_recv()
        sums = scal[it, 0]
        for k in range(1, L * C):
            sums = sums + scal[it, k]
        return jnp.sum(sums[0]), jnp.sum(sums[1])

    vec_s[...] = times_system(rhs)
    copies = share(0, rhs[...], vec_s[...])
    vec_q[...] = times_system(vec_s)
    rr0, curve = collect(0, copies)
    alpha0 = rr0 / curve
    vec_r[...] = rhs[...] - alpha0 * vec_s[...]
    vec_w[...] = vec_s[...] - alpha0 * vec_q[...]
    copies = share(1, vec_r[...], vec_w[...])
    vec_n[...] = times_system(vec_w)
    rr1, curve = collect(1, copies)
    beta1 = rr1 / rr0
    alpha1 = rr1 / (curve - beta1 * rr1 / alpha0)
    last = vec_r[...] - alpha1 * (vec_w[...] + beta1 * vec_s[...])
    copies = share(2, last, vec_w[...] - alpha1 * (vec_n[...] + beta1 * vec_q[...]))
    vec_n[...] = last
    rr2, curve = collect(2, copies)
    beta2 = rr2 / rr1
    alpha2 = rr2 / (curve - beta2 * rr2 / alpha1)
    of_r1 = alpha1 + alpha2 * beta2
    of_r0 = alpha0 + of_r1 * beta1
    out_ref[0] = of_r0 * rhs[...] + of_r1 * vec_r[...] + alpha2 * vec_n[...]

    others = flags.at[pl.ds(1, PLANE * L * C - 1)]
    drain(others, g_recv)
    drain(others, g_send)
    flag_ref[0, 0] = (jnp.max(flags[...]) > 0).astype(jnp.int32)

    for it in range(ITERS):
        for k in range(1, L * C):
            drain(scal.at[it, 0], s_send.at[it, k])
    drain(tok.at[pl.ds(0, 7), pl.ds(0, tokens_here)], ring_send)
    if spare:
        drain(tok.at[pl.ds(0, 7), late_rows], v_send)
    drain(idsb.at[pl.ds(0, 7)], idr_send)
    for s in range(Z):
        drain(feats.at[s, pl.ds(0, (PLANE - 1) * CAP)], f_send.at[s])
        drain(tfin.at[s, pl.ds(0, (PLANE * L * C - 1) * CAP)], t2_send.at[s])
    for n in (1, 2, 3, 4, 7):
        drain(tsend.at[0], t1_send.at[n])
    for n in range(3):
        drain(weights.at[0], w_send.at[n])
    for n in range(Z // 2):
        for k in range(3):
            drain(hid.at[0, pl.ds(0, 2)], h_send.at[n, k])


def refit(limits, number, tokens, expert_ids, targets, gate_weight, up_weight, kept_units):
    most, spare = limits
    tok_rows, model_width = tokens.shape
    routes = expert_ids.shape[1]
    keep = kept_units.shape[1]
    rows, units = gate_weight.shape[1:]
    ids = expert_ids.T
    targets = targets.reshape(-1, model_width)
    part = L * C
    out_cols = model_width // part
    slots = PLANE * CAP
    vmem = pl.BlockSpec(memory_space=pltpu.VMEM)
    hbm = pl.BlockSpec(memory_space=pl.ANY)
    dma = pltpu.SemaphoreType.DMA
    bf, f32 = jnp.bfloat16, jnp.float32
    return pl.pallas_call(
        functools.partial(kernel, limits),
        out_shape=(jax.ShapeDtypeStruct((1, keep, out_cols), f32), jax.ShapeDtypeStruct((1, 1), jnp.int32)),
        in_specs=[vmem, vmem, hbm, hbm, hbm, hbm],
        out_specs=(vmem, pl.BlockSpec(memory_space=pltpu.SMEM)),
        scratch_shapes=[
            pltpu.VMEM((Z, tok_rows + spare, model_width), bf),
            pltpu.VMEM((Z, 8, tok_rows * routes), jnp.int32),
            pltpu.VMEM((tok_rows * routes, model_width), bf),
            pltpu.VMEM((rows, units), bf),
            pltpu.VMEM((rows, units), bf),
            pltpu.VMEM((tok_rows * routes, tok_rows * routes), bf),
            pltpu.VMEM((Z, slots, model_width), bf),
            pltpu.VMEM((Z, slots, model_width), bf),
            pltpu.VMEM((part, 2 * keep, rows), bf),
            pltpu.VMEM((part, Z, keep, slots), bf),
            pltpu.VMEM((Z, most, model_width), bf),
            pltpu.VMEM((Z, most, model_width), bf),
            pltpu.VMEM((Z, part, slots, out_cols), bf),
            pltpu.VMEM((Z, part * slots, out_cols), bf),
            pltpu.VMEM((Z, slots, most + spare), bf),
            pltpu.VMEM((keep, out_cols), f32),
            pltpu.VMEM((keep, keep), f32),
            pltpu.VMEM((keep, out_cols), f32),
            pltpu.VMEM((keep, out_cols), f32),
            pltpu.VMEM((keep, out_cols), f32),
            pltpu.VMEM((keep, out_cols), f32),
            pltpu.VMEM((keep, out_cols), f32),
            pltpu.VMEM((ITERS, part, 2, 8, 128), f32),
            pltpu.VMEM((PLANE * part, 8, 128), f32),
            dma((4,)), dma, dma((5, 2)), dma, dma((5, 2)), dma((Z,)), dma((Z,)), dma((Z,)), dma((Z,)),
            dma((Z,)), dma((Z,)), dma((3,)), dma((3,)), dma((Z // 2, 3)), dma((Z // 2, 3)),
            dma((ITERS, part)), dma((ITERS, part)), dma, dma, dma, dma((5, 2)),
        ],
        compiler_params=pltpu.CompilerParams(
            collective_id=number, has_side_effects=True, vmem_limit_bytes=56 * 2**20
        ),
    )(ids, kept_units, tokens, targets, gate_weight[0], up_weight[0])


def body(*args):
    result, flag = refit((80, 32), 0, *args)
    return lax.cond(flag[0, 0] > 0, lambda: refit((PLANE * CAP, 0), 1, *args)[0], lambda: result)


def solution(mesh):
    placed = (
        P(("expert", "dp"), None),
        P(("expert", "dp"), None),
        P(("expert", "dp"), None, None),
        P("expert", "dp", None),
        P("expert", "dp", None),
        P("expert", None),
    )
    return jax.shard_map(
        body, mesh=mesh, in_specs=placed, out_specs=P("expert", None, "dp"), check_vma=False
    )
```
